32 devices in a mesh: blk: 8 (over y, x, core), dp: 4 (over z).
Axes of the slice: x: 2, y: 2, z: 4, core: 2. Of those that a mesh axis runs over, the one named last changes fastest.
Arguments:
- normed_input: bfloat16 [32, 256, 5120], P(('blk', 'dp')), may hold values from -40 to 40
- segment_ids: int32 [4, 8, 256], P('dp'), may hold values from 0 to 3, never falling along the last dimension, each value on 1 to 128 neighbouring positions
- weights_qkv: bfloat16 [8, 5120, 384], P('blk'), may hold values from -0.08385255 to 0.08385255
- weights_out: bfloat16 [8, 128, 5120], P('blk'), may hold values from -0.5 to 0.5
- cotangent: bfloat16 [32, 256, 5120], P(('blk', 'dp')), may hold values from -6 to 6
Outputs:
- input_grad: bfloat16 [32, 256, 5120], P(('blk', 'dp'))
- grad_qkv: bfloat16 [8, 5120, 384], P('blk', 'dp')
- grad_out: bfloat16 [8, 128, 5120], P('blk', None, 'dp')
The draws below stay inside these ranges and needn't reach their ends.
All inputs are finite; a program needn't handle non-finite values.
Results may differ from the reference program's by a relative error of at most 0.02.
Values may be sent and summed in bfloat16 or wider, within the bound.
A program may use at most 128 MiB of HBM per device.

```python
import math
import jax
import jax.numpy as jnp
import numpy as np
from jax import lax

D = 5120
HD = 128
LEN = 256
GROUPS = 8
SEQS = 32
N_BLK = 8
N_DP = 4


def draw_normed_input(key, part):
    key = jax.random.fold_in(key, 11)
    first = jax.random.fold_in(key, 0)
    base = jax.random.normal(first, (SEQS, LEN, D), jnp.float32)
    return base.astype(jnp.bfloat16)


def draw_weights_qkv(key, part):
    key = jax.random.fold_in(key, 23)
    scale = D ** (-0.5)
    base = jnp.clip(jax.random.normal(key, (GROUPS, D, 3 * HD), jnp.float32), -5.0, 5.0)
    return (base * scale).astype(jnp.bfloat16)


def spiked(result, own_key, source, target, shards_of, factor):
    def block_of(position):
        return (jnp.arange(result.shape[position]) // (result.shape[position] // shards_of)).reshape((-1,) + (1,) * (result.ndim - 1 - position))

    near = jax.random.permutation(own_key, shards_of)[block_of(target)]
    other_side = (block_of(target) + shards_of // 2) % shards_of
    return jnp.where((block_of(source) == near) | (block_of(source) == other_side), factor * result, result)


def block_levels(key, shape, shards, least, high):
    level = 1.0
    for axis_at, parts in shards:
        heights = jax.random.uniform(jax.random.fold_in(jax.random.fold_in(key, 6), axis_at), (parts,), jnp.float32, least / len(shards), high / len(shards))
        level = level * jnp.repeat(jnp.exp(heights), shape[axis_at] // parts).reshape((-1,) + (1,) * (len(shape) - 1 - axis_at))
    return level


def profile(number_of, total, bound, lean):
    loads = [(1 << 20) // math.isqrt(rank ** lean) + 1 for rank in range(2, number_of + 1)]
    rest, given = total - bound - (number_of - 1), [1] * (number_of - 1)
    while rest > 0:
        candidates = [i for i in range(number_of - 1) if given[i] < bound]
        pool, budget = sum([loads[i] for i in candidates]), rest
        for i in candidates:
            more = min(bound - given[i], max(1, budget * loads[i] // pool), rest)
            given[i] = given[i] + more
            rest = rest - more
    return np.array([bound] + given)


def uneven(stream_key, number_of, total, limit, slope):
    if number_of == 2:
        one = jax.random.randint(stream_key, (), max(1, total - limit), min(limit, total - 1) + 1)
        return jnp.stack([one, total - one])
    sizes = jnp.asarray(profile(number_of, total, limit, slope), jnp.int32)
    twos = (number_of - 1) // 2
    donor, receiver = sizes[1:1 + 2 * twos:2], sizes[2:2 + 2 * twos:2]
    slack = jnp.minimum(donor - 1, limit - receiver)
    moved = jax.random.randint(jax.random.fold_in(stream_key, 1), (twos,), 0, 1 << 20) % (slack + 1)
    sizes = sizes.at[1:1 + 2 * twos:2].set(donor - moved).at[2:2 + 2 * twos:2].set(receiver + moved)
    return sizes[jax.random.permutation(jax.random.fold_in(stream_key, 2), number_of)]


def noise(own_key, shape, scale, most, cuts=(), kind=jnp.bfloat16):
    array = scale * jax.random.normal(own_key, shape, jnp.float32)
    if cuts:
        array = array * block_levels(own_key, shape, cuts, -0.22, 0.18)
    return jnp.clip(array, -most, most).astype(kind)


def noise_with(stream_key, shape, width, bound, cuts, heavy, held_as=jnp.bfloat16):
    entries = width * jax.random.normal(stream_key, shape, jnp.float32)
    if cuts:
        entries = entries * block_levels(stream_key, shape, cuts, -0.22, 0.18)
    return jnp.clip(spiked(entries, jax.random.fold_in(stream_key, 3), *heavy), -bound, bound).astype(held_as)


def setup_inputs(seed: int = 0) -> dict:
    seeds = jax.random.split(jax.random.key(seed), 6)
    return {
        "normed_input": draw_normed_input(jax.random.fold_in(seeds[5], 71), 0),
        "segment_ids": jax.vmap(lambda own: jnp.searchsorted(jnp.cumsum(uneven(own, 4, LEN, LEN // 2, 1)), jnp.arange(LEN), side="right"))(jax.random.split(seeds[1], N_DP * N_BLK)).reshape((N_DP, N_BLK, LEN)).astype(jnp.int32),
        "weights_qkv": draw_weights_qkv(jax.random.fold_in(seeds[5], 71), 0),
        "weights_out": noise(seeds[3], (GROUPS, HD, D), HD ** -0.5, 0.5, ((0, 8),)),
        "cotangent": noise_with(seeds[4], (SEQS, LEN, D), 1.0, 6.0, ((0, 32),), (0, 2, 32, 2.75)),
    }


def group_terms(inputs, seg_row, w_qkv, w_out, grad_in):
    head = w_out.shape[0]
    scale = head ** -0.5
    qkv = jnp.dot(inputs, w_qkv, preferred_element_type=jnp.float32).astype(jnp.bfloat16)
    query = qkv[:, :head]
    keys = qkv[:, head:2 * head]
    values = qkv[:, 2 * head:]
    count = inputs.shape[0]
    places = jnp.arange(count, dtype=jnp.int32)
    allowed = (places[:, None] >= places[None, :]) & (seg_row[:, None] == seg_row[None, :])
    scores = jnp.dot(query, keys.T, preferred_element_type=jnp.float32) * scale
    scores = jnp.where(allowed, scores, jnp.float32(-1e30))
    top = jnp.max(scores, axis=-1, keepdims=True)
    expo = jnp.where(allowed, jnp.exp(scores - top), jnp.float32(0.0))
    probs = expo / jnp.sum(expo, axis=-1, keepdims=True)
    probs_b = probs.astype(jnp.bfloat16)
    attended = jnp.dot(probs_b, values, preferred_element_type=jnp.float32).astype(jnp.bfloat16)
    grad_wout = jnp.dot(attended.T, grad_in, preferred_element_type=jnp.float32)
    d_att = jnp.dot(grad_in, w_out.T, preferred_element_type=jnp.float32).astype(jnp.bfloat16)
    d_probs = jnp.dot(d_att, values.T, preferred_element_type=jnp.float32)
    d_scores = (probs * (d_probs - jnp.sum(probs * d_probs, axis=-1, keepdims=True)) * scale).astype(jnp.bfloat16)
    d_query = jnp.dot(d_scores, keys, preferred_element_type=jnp.float32)
    d_keys = jnp.dot(d_scores.T, query, preferred_element_type=jnp.float32)
    d_values = jnp.dot(probs_b.T, d_att, preferred_element_type=jnp.float32)
    d_qkv = jnp.concatenate([d_query, d_keys, d_values], axis=1).astype(jnp.bfloat16)
    grad_wqkv = jnp.dot(inputs.T, d_qkv, preferred_element_type=jnp.float32)
    input_term = jnp.dot(d_qkv, w_qkv.T, preferred_element_type=jnp.float32)
    return input_term, grad_wqkv, grad_wout


def reference(normed_input, segment_ids, weights_qkv, weights_out, cotangent):
    total = normed_input.shape[0]

    def visit(carry, index):
        acc_qkv, acc_out = carry
        cycle_pos = index // N_DP
        cycle = index % N_DP
        prev = (cycle_pos + N_BLK - 1) % N_BLK
        inputs = normed_input[index]
        grad_in = cotangent[index]
        seg_row = segment_ids[cycle, cycle_pos]
        term_a, gq_a, go_a = group_terms(inputs, seg_row, weights_qkv[cycle_pos], weights_out[cycle_pos], grad_in)
        term_b, gq_b, go_b = group_terms(inputs, seg_row, weights_qkv[prev], weights_out[prev], grad_in)
        acc_qkv = acc_qkv.at[cycle_pos].add(gq_a).at[prev].add(gq_b)
        acc_out = acc_out.at[cycle_pos].add(go_a).at[prev].add(go_b)
        return (acc_qkv, acc_out), (term_a + term_b).astype(jnp.bfloat16)

    start = (jnp.zeros(weights_qkv.shape, jnp.float32), jnp.zeros(weights_out.shape, jnp.float32))
    (acc_qkv, acc_out), input_grad = lax.scan(visit, start, jnp.arange(total, dtype=jnp.int32))
    return input_grad, acc_qkv.astype(jnp.bfloat16), acc_out.astype(jnp.bfloat16)
```

```python
import functools

import jax
import jax.numpy as jnp
from jax import lax
from jax.experimental import pallas as pl
from jax.experimental.pallas import tpu as pltpu
from jax.sharding import PartitionSpec as P

MESH = pl.DeviceIdType.MESH
F32 = jnp.float32
BF16 = jnp.bfloat16
PARTS = 2


def dot(a, b):
    return jnp.dot(a, b, preferred_element_type=F32)


def dot_nt(a, b):
    return lax.dot_general(a, b, (((1,), (1,)), ((), ())), preferred_element_type=F32)


def dot_tn(a, b):
    return lax.dot_general(a, b, (((0,), (0,)), ((), ())), preferred_element_type=F32)


def attention_terms(qkv, d_att, seg_row, head):
    scale = head ** (-0.5)
    query, keys, values = qkv[:, :head], qkv[:, head : 2 * head], qkv[:, 2 * head :]
    count = qkv.shape[0]
    seg_rows = jnp.broadcast_to(seg_row.astype(F32), (count, count))
    places = lax.broadcasted_iota(jnp.int32, (count, count), 0)
    others = lax.broadcasted_iota(jnp.int32, (count, count), 1)
    allowed = (places >= others) & (seg_rows.T == seg_rows)
    scores = jnp.where(allowed, dot_nt(query, keys) * scale, F32(-1e30))
    top = jnp.max(scores, axis=-1, keepdims=True)
    expo = jnp.where(allowed, jnp.exp(scores - top), F32(0.0))
    probs = expo / jnp.sum(expo, axis=-1, keepdims=True)
    probs_b = probs.astype(BF16)
    attended = dot(probs_b, values).astype(BF16)
    d_probs = dot_nt(d_att, values)
    d_scores = (probs * (d_probs - jnp.sum(probs * d_probs, axis=-1, keepdims=True)) * scale).astype(BF16)
    d_qkv = jnp.concatenate([dot(d_scores, keys), dot_tn(d_scores, query), dot_tn(probs_b, d_att)], axis=1)
    return d_qkv.astype(BF16), attended


def kernel(
    nb, n, wide, x_hbm, g_hbm, seg_ref, w_hbm, wo_hbm, ig_ref, gs_ref,
    x, g, xf, gf, w, wo, dt, dq, gt, from_low, from_high, term, tsend, tback,
    load_sem, out_send, out_recv, t_send, t_recv, up_send, up_recv, down_send, down_recv,
):
    b, d = lax.axis_index("blk"), lax.axis_index("dp")
    nxt, prv = lax.rem(b + 1, nb), lax.rem(b + nb - 1, nb)
    head = wo.shape[0]
    cols = 3 * head
    part = (cols + head) // PARTS

    loads = [
        pltpu.make_async_copy(src, dst, load_sem.at[i])
        for i, (src, dst) in enumerate(((x_hbm, x), (w_hbm, w), (g_hbm, g), (wo_hbm, wo)))
    ]
    for load in loads:
        load.start()

    barrier = pltpu.get_barrier_semaphore()
    for other in (nxt, prv):
        pl.semaphore_signal(barrier, inc=1, device_id={"blk": other}, device_id_type=MESH)

    @pl.when(d > 0)
    def _():
        pl.semaphore_signal(barrier, inc=1, device_id={"dp": d - 1}, device_id_type=MESH)

    @pl.when(d < n - 1)
    def _():
        pl.semaphore_signal(barrier, inc=1, device_id={"dp": d + 1}, device_id_type=MESH)

    pl.semaphore_wait(barrier, 2 + (d > 0).astype(jnp.int32) + (d < n - 1).astype(jnp.int32))

    def lanes(c):
        return pl.ds(pl.multiple_of(c * wide, 128), wide)

    def send_out(which, c):
        src, dst = ((x_hbm, xf), (g_hbm, gf))[which]
        return pltpu.make_async_remote_copy(
            src_ref=src.at[:, lanes(c)], dst_ref=dst.at[:, lanes(c)],
            send_sem=out_send.at[which, c], recv_sem=out_recv.at[which, c],
            device_id={"blk": prv}, device_id_type=MESH,
        )

    def send_term(c):
        return pltpu.make_async_remote_copy(
            src_ref=tsend.at[:, lanes(c)], dst_ref=tback.at[:, lanes(c)],
            send_sem=t_send.at[c], recv_sem=t_recv.at[c],
            device_id={"blk": nxt}, device_id_type=MESH,
        )

    def rows(p):
        return pl.ds(p * part, part)

    def send_up(k, p):
        return pltpu.make_async_remote_copy(
            src_ref=gt.at[k, rows(p)], dst_ref=from_low.at[k, rows(p)],
            send_sem=up_send.at[k, p], recv_sem=up_recv.at[k, p],
            device_id={"dp": d + 1}, device_id_type=MESH,
        )

    def send_down(k, p):
        return pltpu.make_async_remote_copy(
            src_ref=gt.at[k, rows(p)], dst_ref=from_high.at[k, rows(p)],
            send_sem=down_send.at[k, p], recv_sem=down_recv.at[k, p],
            device_id={"dp": d - 1}, device_id_type=MESH,
        )

    for which in range(2):
        for c in range(n):
            send_out(which, c).start()

    def differentiate(slot, x_ref, g_ref, wait_x, wait_g, seg_at):
        def qkv_step(c, total):
            wait_x(c)
            return total + dot(x_ref[:, lanes(c)], w[lanes(c), :])

        def att_step(c, total):
            wait_g(c)
            return total + dot_nt(g_ref[:, lanes(c)], wo[:, lanes(c)])

        count = x_ref.shape[0]
        qkv = lax.fori_loop(0, n, qkv_step, jnp.zeros((count, cols), F32)).astype(BF16)
        d_att = lax.fori_loop(0, n, att_step, jnp.zeros((count, head), F32)).astype(BF16)
        d_qkv, attended = attention_terms(qkv, d_att, seg_ref[pl.ds(seg_at, 1), :], head)
        dq[slot] = d_qkv
        dt[slot, :cols, :] = d_qkv.astype(F32).T.astype(BF16)
        dt[slot, cols:, :] = attended.astype(F32).T.astype(BF16)

    for load in loads:
        load.wait()
    differentiate(0, x, g, lambda c: None, lambda c: None, b)

    def own_term(c, carry):
        term[:, lanes(c)] = dot_nt(dq[0], w[lanes(c), :])
        return carry

    lax.fori_loop(0, n, own_term, 0)

    differentiate(
        1, xf, gf, lambda c: send_out(0, c).wait_recv(), lambda c: send_out(1, c).wait_recv(), nxt
    )

    def gradient(c, carry):
        gt[c, :cols, :] = (dot(dt[0, :cols, :], x[:, lanes(c)]) + dot(dt[1, :cols, :], xf[:, lanes(c)])).astype(BF16)
        gt[c, cols:, :] = (dot(dt[0, cols:, :], g[:, lanes(c)]) + dot(dt[1, cols:, :], gf[:, lanes(c)])).astype(BF16)
        return carry

    lax.fori_loop(0, n, gradient, 0)

    @pl.when(d == 0)
    def _():
        for k in range(n - 1, 0, -1):
            for p in range(PARTS):
                send_up(k, p).start()

    @pl.when(d == n - 1)
    def _():
        for k in range(n - 1):
            for p in range(PARTS):
                send_down(k, p).start()

    def far_term(c, carry):
        tsend[:, lanes(c)] = dot_nt(dq[1], w[lanes(c), :]).astype(BF16)
        send_term(c).start()
        return carry

    lax.fori_loop(0, n, far_term, 0)

    for j in range(n - 1):
        for p in range(PARTS):
            up, down = n - 1 - j, j

            @pl.when((d > 0) & (d < up))
            def _(up=up, p=p):
                send_up(up, p).wait_recv()
                gt[up, rows(p), :] = (gt[up, rows(p), :].astype(F32) + from_low[up, rows(p), :].astype(F32)).astype(BF16)
                send_up(up, p).start()

            @pl.when((d < n - 1) & (d > down))
            def _(down=down, p=p):
                send_down(down, p).wait_recv()
                gt[down, rows(p), :] = (
                    gt[down, rows(p), :].astype(F32) + from_high[down, rows(p), :].astype(F32)
                ).astype(BF16)
                send_down(down, p).start()

    def finish_input(c, carry):
        send_term(c).wait_recv()
        ig_ref[:, lanes(c)] = (term[:, lanes(c)] + tback[:, lanes(c)].astype(F32)).astype(BF16)
        return carry

    lax.fori_loop(0, n, finish_input, 0)

    for p in range(PARTS):

        @pl.when(d == 0)
        def _(p=p):
            send_down(d, p).wait_recv()
            gs_ref[rows(p), :] = (gt[d, rows(p), :].astype(F32) + from_high[d, rows(p), :].astype(F32)).astype(BF16)

        @pl.when(d == n - 1)
        def _(p=p):
            send_up(d, p).wait_recv()
            gs_ref[rows(p), :] = (gt[d, rows(p), :].astype(F32) + from_low[d, rows(p), :].astype(F32)).astype(BF16)

        @pl.when((d > 0) & (d < n - 1))
        def _(p=p):
            send_down(d, p).wait_recv()
            send_up(d, p).wait_recv()
            gs_ref[rows(p), :] = (
                gt[d, rows(p), :].astype(F32) + from_low[d, rows(p), :].astype(F32) + from_high[d, rows(p), :].astype(F32)
            ).astype(BF16)

    for c in range(n):
        send_out(0, c).wait_send()
        send_out(1, c).wait_send()
        send_term(c).wait_send()
        for p in range(PARTS):

            @pl.when(d < c)
            def _(c=c, p=p):
                send_up(c, p).wait_send()

            @pl.when(d > c)
            def _(c=c, p=p):
                send_down(c, p).wait_send()


def spread(array, dim, n, wide):
    shape = array.shape
    each = shape[dim] // n
    if each == wide:
        return array
    split = array.reshape(shape[:dim] + (n, each) + shape[dim + 1 :])
    pads = [(0, 0)] * split.ndim
    pads[dim + 1] = (0, wide - each)
    return jnp.pad(split, pads).reshape(shape[:dim] + (n * wide,) + shape[dim + 1 :])


def local(normed_input, segment_ids, weights_qkv, weights_out, cotangent):
    nb, n = lax.axis_size("blk"), lax.axis_size("dp")
    _, count, depth = normed_input.shape
    head = weights_out.shape[1]
    each = depth // n
    wide = -(-each // 128) * 128
    full = n * wide
    rows = 4 * head
    hbm = pl.BlockSpec(memory_space=pl.ANY)
    vmem = pl.BlockSpec(memory_space=pltpu.VMEM)
    dma = pltpu.SemaphoreType.DMA
    seq = pltpu.VMEM((count, full), BF16)
    shards = pltpu.VMEM((n, rows, wide), BF16)
    input_grad, summed = pl.pallas_call(
        functools.partial(kernel, nb, n, wide),
        out_shape=(jax.ShapeDtypeStruct((count, full), BF16), jax.ShapeDtypeStruct((rows, wide), BF16)),
        in_specs=[hbm, hbm, vmem, hbm, hbm],
        out_specs=(vmem, vmem),
        scratch_shapes=[
            seq, seq, seq, seq,
            pltpu.VMEM((full, 3 * head), BF16),
            pltpu.VMEM((head, full), BF16),
            pltpu.VMEM((2, rows, count), BF16),
            pltpu.VMEM((2, count, 3 * head), BF16),
            shards, shards, shards,
            pltpu.VMEM((count, full), F32),
            seq, seq,
            dma((4,)), dma((2, n)), dma((2, n)), dma((n,)), dma((n,)),
            dma((n, PARTS)), dma((n, PARTS)), dma((n, PARTS)), dma((n, PARTS)),
        ],
        compiler_params=pltpu.CompilerParams(
            collective_id=0, has_side_effects=True, vmem_limit_bytes=60 * 1024 * 1024
        ),
    )(
        spread(normed_input[0], 1, n, wide),
        spread(cotangent[0], 1, n, wide),
        segment_ids[0],
        spread(weights_qkv[0], 0, n, wide),
        spread(weights_out[0], 1, n, wide),
    )
    if each != wide:
        input_grad = input_grad.reshape(count, n, wide)[:, :, :each].reshape(count, depth)
        summed = summed[:, :each]
    return input_grad[None], summed[: 3 * head].T[None], summed[3 * head :][None]


def solution(mesh):
    placed = (
        P(("blk", "dp"), None, None),
        P("dp", None, None),
        P("blk", None, None),
        P("blk", None, None),
        P(("blk", "dp"), None, None),
    )
    return jax.shard_map(
        local,
        mesh=mesh,
        in_specs=placed,
        out_specs=(P(("blk", "dp"), None, None), P("blk", "dp", None), P("blk", None, "dp")),
        check_vma=False,
    )
```

```python
import functools

import jax
import jax.numpy as jnp
from jax import lax
from jax.experimental import pallas as pl
from jax.experimental.pallas import tpu as pltpu
from jax.sharding import PartitionSpec as P

MESH = pl.DeviceIdType.MESH
F32 = jnp.float32
BF16 = jnp.bfloat16
PARTS = 4


def dot(a, b):
    return jnp.dot(a, b, preferred_element_type=F32)


def dot_nt(a, b):
    return lax.dot_general(a, b, (((1,), (1,)), ((), ())), preferred_element_type=F32)


def dot_tn(a, b):
    return lax.dot_general(a, b, (((0,), (0,)), ((), ())), preferred_element_type=F32)


def attention_terms(qkv, d_att, seg_row, head):
    scale = head ** (-0.5)
    query, keys, values = qkv[:, :head], qkv[:, head : 2 * head], qkv[:, 2 * head :]
    count = qkv.shape[0]
    seg_rows = jnp.broadcast_to(seg_row.astype(F32), (count, count))
    places = lax.broadcasted_iota(jnp.int32, (count, count), 0)
    others = lax.broadcasted_iota(jnp.int32, (count, count), 1)
    allowed = (places >= others) & (seg_rows.T == seg_rows)
    scores = jnp.where(allowed, dot_nt(query, keys) * scale, F32(-1e30))
    top = jnp.max(scores, axis=-1, keepdims=True)
    expo = jnp.where(allowed, jnp.exp(scores - top), F32(0.0))
    probs = expo / jnp.sum(expo, axis=-1, keepdims=True)
    probs_b = probs.astype(BF16)
    attended = dot(probs_b, values).astype(BF16)
    d_probs = dot_nt(d_att, values)
    d_scores = (probs * (d_probs - jnp.sum(probs * d_probs, axis=-1, keepdims=True)) * scale).astype(BF16)
    d_qkv = jnp.concatenate([dot(d_scores, keys), dot_tn(d_scores, query), dot_tn(probs_b, d_att)], axis=1)
    return d_qkv.astype(BF16), attended


def kernel(
    nb, n, wide, x_hbm, g_hbm, seg_ref, w_hbm, wo_hbm, ig_hbm, gs_ref,
    xx, gg, w, wo, dt, dq, gt, from_low, from_high, term, tsend, tback,
    load_sem, out_send, out_recv, t_send, t_recv, up_send, up_recv, down_send, down_recv, store_sem,
):
    b, d = lax.axis_index("blk"), lax.axis_index("dp")
    nxt, prv = lax.rem(b + 1, nb), lax.rem(b + nb - 1, nb)
    head = wo.shape[0]
    cols = 3 * head
    count = tsend.shape[0]
    part = (cols + head) // PARTS
    own, far = pl.ds(0, count), pl.ds(count, count)

    loads = [
        pltpu.make_async_copy(src, dst, load_sem.at[i])
        for i, (src, dst) in enumerate(((x_hbm, xx.at[own]), (w_hbm, w), (g_hbm, gg.at[own]), (wo_hbm, wo)))
    ]
    for load in loads:
        load.start()

    barrier = pltpu.get_barrier_semaphore()
    for other in (nxt, prv):
        pl.semaphore_signal(barrier, inc=1, device_id={"blk": other}, device_id_type=MESH)

    @pl.when(d > 0)
    def _():
        pl.semaphore_signal(barrier, inc=1, device_id={"dp": d - 1}, device_id_type=MESH)

    @pl.when(d < n - 1)
    def _():
        pl.semaphore_signal(barrier, inc=1, device_id={"dp": d + 1}, device_id_type=MESH)

    pl.semaphore_wait(barrier, 2 + (d > 0).astype(jnp.int32) + (d < n - 1).astype(jnp.int32))

    def lanes(c):
        return pl.ds(pl.multiple_of(c * wide, 128), wide)

    def send_out(which, c):
        src, dst = ((x_hbm, xx), (g_hbm, gg))[which]
        return pltpu.make_async_remote_copy(
            src_ref=src.at[:, lanes(c)], dst_ref=dst.at[far, lanes(c)],
            send_sem=out_send.at[which, c], recv_sem=out_recv.at[which, c],
            device_id={"blk": prv}, device_id_type=MESH,
        )

    def send_term(c):
        return pltpu.make_async_remote_copy(
            src_ref=tsend.at[:, lanes(c)], dst_ref=tback.at[:, lanes(c)],
            send_sem=t_send.at[c], recv_sem=t_recv.at[c],
            device_id={"blk": nxt}, device_id_type=MESH,
        )

    def rows(p):
        return pl.ds(pl.multiple_of(p * part, part), part)

    def send_up(k, p):
        return pltpu.make_async_remote_copy(
            src_ref=gt.at[k, rows(p)], dst_ref=from_low.at[k, rows(p)],
            send_sem=up_send.at[k, p], recv_sem=up_recv.at[k, p],
            device_id={"dp": d + 1}, device_id_type=MESH,
        )

    def send_down(k, p):
        return pltpu.make_async_remote_copy(
            src_ref=gt.at[k, rows(p)], dst_ref=from_high.at[k, rows(p)],
            send_sem=down_send.at[k, p], recv_sem=down_recv.at[k, p],
            device_id={"dp": d - 1}, device_id_type=MESH,
        )

    for which in range(2):
        for c in range(n):
            send_out(which, c).start()

    def differentiate(slot, at, wait_x, wait_g, seg_at):
        def qkv_step(c, total):
            wait_x(c)
            return total + dot(xx[at, lanes(c)], w[lanes(c), :])

        def att_step(c, total):
            wait_g(c)
            return total + dot_nt(gg[at, lanes(c)], wo[:, lanes(c)])

        qkv = lax.fori_loop(0, n, qkv_step, jnp.zeros((count, cols), F32)).astype(BF16)
        d_att = lax.fori_loop(0, n, att_step, jnp.zeros((count, head), F32)).astype(BF16)
        d_qkv, attended = attention_terms(qkv, d_att, seg_ref[pl.ds(seg_at, 1), :], head)
        dq[slot] = d_qkv
        dt[:cols, at] = d_qkv.astype(F32).T.astype(BF16)
        dt[cols:, at] = attended.astype(F32).T.astype(BF16)

    for load in loads:
        load.wait()
    differentiate(0, own, lambda c: None, lambda c: None, b)

    def own_term(c, carry):
        term[:, lanes(c)] = dot_nt(dq[0], w[lanes(c), :])
        return carry

    lax.fori_loop(0, n, own_term, 0)

    differentiate(1, far, lambda c: send_out(0, c).wait_recv(), lambda c: send_out(1, c).wait_recv(), nxt)

    def gradient(i, carry):
        k = jnp.where(d == n - 1, i, n - 1 - i)
        gt[k, :cols, :] = dot(dt[:cols, :], xx[:, lanes(k)]).astype(BF16)
        gt[k, cols:, :] = dot(dt[cols:, :], gg[:, lanes(k)]).astype(BF16)

        @pl.when((d == 0) & (k > 0))
        def _():
            for p in range(PARTS):
                send_up(k, p).start()

        @pl.when((d == n - 1) & (k < n - 1))
        def _():
            for p in range(PARTS):
                send_down(k, p).start()

        return carry

    lax.fori_loop(0, n, gradient, 0)

    def far_term(c, carry):
        tsend[:, lanes(c)] = dot_nt(dq[1], w[lanes(c), :]).astype(BF16)
        send_term(c).start()
        return carry

    lax.fori_loop(0, n, far_term, 0)

    def tick(t, carry):
        up, down = t - d, t - (n - 1 - d)

        @pl.when((d > 0) & (up >= 0) & (up < (n - 1 - d) * PARTS))
        def _():
            k, p = n - 1 - up // PARTS, up % PARTS
            send_up(k, p).wait_recv()
            gt[k, rows(p), :] = (gt[k, rows(p), :].astype(F32) + from_low[k, rows(p), :].astype(F32)).astype(BF16)
            send_up(k, p).start()

        @pl.when((d < n - 1) & (down >= 0) & (down < d * PARTS))
        def _():
            k, p = down // PARTS, down % PARTS
            send_down(k, p).wait_recv()
            gt[k, rows(p), :] = (gt[k, rows(p), :].astype(F32) + from_high[k, rows(p), :].astype(F32)).astype(BF16)
            send_down(k, p).start()

        return carry

    lax.fori_loop(1, 1 + (n - 2) * PARTS, tick, 0)

    def store(c):
        return pltpu.make_async_copy(tback.at[:, lanes(c)], ig_hbm.at[:, lanes(c)], store_sem.at[c])

    def finish_input(c, carry):
        send_term(c).wait_recv()
        tback[:, lanes(c)] = (term[:, lanes(c)] + tback[:, lanes(c)].astype(F32)).astype(BF16)
        store(c).start()
        return carry

    lax.fori_loop(0, n, finish_input, 0)

    for p in range(PARTS):

        @pl.when(d == 0)
        def _(p=p):
            send_down(d, p).wait_recv()
            gs_ref[rows(p), :] = (gt[d, rows(p), :].astype(F32) + from_high[d, rows(p), :].astype(F32)).astype(BF16)

        @pl.when(d == n - 1)
        def _(p=p):
            send_up(d, p).wait_recv()
            gs_ref[rows(p), :] = (gt[d, rows(p), :].astype(F32) + from_low[d, rows(p), :].astype(F32)).astype(BF16)

        @pl.when((d > 0) & (d < n - 1))
        def _(p=p):
            send_down(d, p).wait_recv()
            send_up(d, p).wait_recv()
            gs_ref[rows(p), :] = (
                gt[d, rows(p), :].astype(F32) + from_low[d, rows(p), :].astype(F32) + from_high[d, rows(p), :].astype(F32)
            ).astype(BF16)

    for c in range(n):
        send_out(0, c).wait_send()
        send_out(1, c).wait_send()
        send_term(c).wait_send()
        store(c).wait()
        for p in range(PARTS):

            @pl.when(d < c)
            def _(c=c, p=p):
                send_up(c, p).wait_send()

            @pl.when(d > c)
            def _(c=c, p=p):
                send_down(c, p).wait_send()


def place_kernel(n, wide, ig_hbm, gs_hbm, out_ig, out_qkv, out_out, shard, turned, ig, sem):
    cols = turned.shape[1]

    def lanes(c):
        return pl.ds(c * wide, wide)

    fetch = pltpu.make_async_copy(gs_hbm, shard, sem.at[0])
    fetch.start()
    reads = [pltpu.make_async_copy(ig_hbm.at[:, lanes(c)], ig.at[:, lanes(c)], sem.at[3 + c]) for c in range(n)]
    writes = [pltpu.make_async_copy(ig.at[:, lanes(c)], out_ig.at[:, lanes(c)], sem.at[3 + n + c]) for c in range(n)]
    for read in reads:
        read.start()
    fetch.wait()
    plain = pltpu.make_async_copy(shard.at[pl.ds(cols, shard.shape[0] - cols)], out_out, sem.at[1])
    plain.start()
    for read, write in zip(reads, writes):
        read.wait()
        write.start()
    turned[...] = shard[:cols, :].astype(F32).T.astype(BF16)
    across = pltpu.make_async_copy(turned, out_qkv, sem.at[2])
    across.start()
    plain.wait()
    across.wait()
    for write in writes:
        write.wait()


def spread(array, dim, n, wide):
    shape = array.shape
    each = shape[dim] // n
    if each == wide:
        return array
    split = array.reshape(shape[:dim] + (n, each) + shape[dim + 1 :])
    pads = [(0, 0)] * split.ndim
    pads[dim + 1] = (0, wide - each)
    return jnp.pad(split, pads).reshape(shape[:dim] + (n * wide,) + shape[dim + 1 :])


def local(normed_input, segment_ids, weights_qkv, weights_out, cotangent):
    nb, n = lax.axis_size("blk"), lax.axis_size("dp")
    _, count, depth = normed_input.shape
    head = weights_out.shape[1]
    each = depth // n
    wide = -(-each // 128) * 128
    full = n * wide
    rows = 4 * head
    hbm = pl.BlockSpec(memory_space=pl.ANY)
    vmem = pl.BlockSpec(memory_space=pltpu.VMEM)
    dma = pltpu.SemaphoreType.DMA
    seq = pltpu.VMEM((count, full), BF16)
    pairs = pltpu.VMEM((2 * count, full), BF16)
    shards = pltpu.VMEM((n, rows, wide), BF16)
    input_grad, summed = pl.pallas_call(
        functools.partial(kernel, nb, n, wide),
        out_shape=(jax.ShapeDtypeStruct((count, full), BF16), jax.ShapeDtypeStruct((rows, wide), BF16)),
        in_specs=[hbm, hbm, vmem, hbm, hbm],
        out_specs=(hbm, vmem),
        scratch_shapes=[
            pairs, pairs,
            pltpu.VMEM((full, 3 * head), BF16),
            pltpu.VMEM((head, full), BF16),
            pltpu.VMEM((rows, 2 * count), BF16),
            pltpu.VMEM((2, count, 3 * head), BF16),
            shards, shards, shards,
            pltpu.VMEM((count, full), F32),
            seq, seq,
            dma((4,)), dma((2, n)), dma((2, n)), dma((n,)), dma((n,)),
            dma((n, PARTS)), dma((n, PARTS)), dma((n, PARTS)), dma((n, PARTS)), dma((n,)),
        ],
        compiler_params=pltpu.CompilerParams(
            collective_id=0, has_side_effects=True, vmem_limit_bytes=60 * 1024 * 1024
        ),
    )(
        spread(normed_input[0], 1, n, wide),
        spread(cotangent[0], 1, n, wide),
        segment_ids[0],
        spread(weights_qkv[0], 0, n, wide),
        spread(weights_out[0], 1, n, wide),
    )
    input_grad, grad_qkv, grad_out = pl.pallas_call(
        functools.partial(place_kernel, n, wide),
        out_shape=(
            jax.ShapeDtypeStruct((count, full), BF16),
            jax.ShapeDtypeStruct((wide, 3 * head), BF16),
            jax.ShapeDtypeStruct((head, wide), BF16),
        ),
        in_specs=[hbm, hbm],
        out_specs=(hbm, hbm, hbm),
        scratch_shapes=[
            pltpu.VMEM((rows, wide), BF16),
            pltpu.VMEM((wide, 3 * head), BF16),
            pltpu.VMEM((count, full), BF16),
            dma((3 + 2 * n,)),
        ],
        compiler_params=pltpu.CompilerParams(vmem_limit_bytes=60 * 1024 * 1024),
    )(input_grad, summed)
    if each != wide:
        input_grad = input_grad.reshape(count, n, wide)[:, :, :each].reshape(count, depth)
    return input_grad[None], grad_qkv[None, :each], grad_out[None, :, :each]


def solution(mesh):
    placed = (
        P(("blk", "dp"), None, None),
        P("dp", None, None),
        P("blk", None, None),
        P("blk", None, None),
        P(("blk", "dp"), None, None),
    )
    return jax.shard_map(
        local,
        mesh=mesh,
        in_specs=placed,
        out_specs=(P(("blk", "dp"), None, None), P("blk", "dp", None), P("blk", None, "dp")),
        check_vma=False,
    )
```

```python
import functools

import jax
import jax.numpy as jnp
from jax import lax
from jax.experimental import pallas as pl
from jax.experimental.pallas import tpu as pltpu
from jax.sharding import PartitionSpec as P

MESH = pl.DeviceIdType.MESH
F32 = jnp.float32
BF16 = jnp.bfloat16
PARTS = 4


def dot(a, b):
    return jnp.dot(a, b, preferred_element_type=F32)


def dot_nt(a, b):
    return lax.dot_general(a, b, (((1,), (1,)), ((), ())), preferred_element_type=F32)


def dot_tn(a, b):
    return lax.dot_general(a, b, (((0,), (0,)), ((), ())), preferred_element_type=F32)


def attention_terms(qkv, d_att_of, seg_row, head):
    scale = head ** (-0.5)
    query, keys, values = qkv[:, :head], qkv[:, head : 2 * head], qkv[:, 2 * head :]
    count = qkv.shape[0]
    seg_rows = jnp.broadcast_to(seg_row.astype(F32), (count, count))
    places = lax.broadcasted_iota(jnp.int32, (count, count), 0)
    others = lax.broadcasted_iota(jnp.int32, (count, count), 1)
    allowed = (places >= others) & (seg_rows.T == seg_rows)
    scores = jnp.where(allowed, dot_nt(query, keys) * scale, F32(-1e30))
    top = jnp.max(scores, axis=-1, keepdims=True)
    expo = jnp.where(allowed, jnp.exp(scores - top), F32(0.0))
    probs = expo / jnp.sum(expo, axis=-1, keepdims=True)
    probs_b = probs.astype(BF16)
    attended = dot(probs_b, values).astype(BF16)
    d_att = d_att_of()
    d_probs = dot_nt(d_att, values)
    d_scores = (probs * (d_probs - jnp.sum(probs * d_probs, axis=-1, keepdims=True)) * scale).astype(BF16)
    d_qkv = jnp.concatenate([dot(d_scores, keys), dot_tn(d_scores, query), dot_tn(probs_b, d_att)], axis=1)
    return d_qkv.astype(BF16), attended


def kernel(
    nb, n, wide, x_hbm, g_hbm, seg_ref, w_hbm, wo_hbm, ig_hbm, gs_ref,
    xx, gg, w, wo, wo_prev, att_to, att_from, dt, dq, gt, from_low, from_high, term, tsend, tback,
    load_sem, out_send, out_recv, wo_sem, att_sem, t_send, t_recv, up_send, up_recv, down_send, down_recv, store_sem,
):
    b, d = lax.axis_index("blk"), lax.axis_index("dp")
    nxt, prv = lax.rem(b + 1, nb), lax.rem(b + nb - 1, nb)
    head = wo.shape[0]
    cols = 3 * head
    count = tsend.shape[0]
    part = (cols + head) // PARTS
    own, far = pl.ds(0, count), pl.ds(count, count)

    loads = [
        pltpu.make_async_copy(src, dst, load_sem.at[i])
        for i, (src, dst) in enumerate(((x_hbm, xx.at[own]), (w_hbm, w), (g_hbm, gg.at[own]), (wo_hbm, wo)))
    ]
    for load in loads:
        load.start()

    barrier = pltpu.get_barrier_semaphore()
    for other in (nxt, prv):
        pl.semaphore_signal(barrier, inc=1, device_id={"blk": other}, device_id_type=MESH)

    @pl.when(d > 0)
    def _():
        pl.semaphore_signal(barrier, inc=1, device_id={"dp": d - 1}, device_id_type=MESH)

    @pl.when(d < n - 1)
    def _():
        pl.semaphore_signal(barrier, inc=1, device_id={"dp": d + 1}, device_id_type=MESH)

    pl.semaphore_wait(barrier, 2 + (d > 0).astype(jnp.int32) + (d < n - 1).astype(jnp.int32))

    def lanes(c):
        return pl.ds(pl.multiple_of(c * wide, 128), wide)

    def send_out(which, c):
        src, dst = ((x_hbm, xx), (g_hbm, gg))[which]
        return pltpu.make_async_remote_copy(
            src_ref=src.at[:, lanes(c)], dst_ref=dst.at[far, lanes(c)],
            send_sem=out_send.at[which, c], recv_sem=out_recv.at[which, c],
            device_id={"blk": prv}, device_id_type=MESH,
        )

    def send_term(c):
        return pltpu.make_async_remote_copy(
            src_ref=tsend.at[:, lanes(c)], dst_ref=tback.at[:, lanes(c)],
            send_sem=t_send.at[c], recv_sem=t_recv.at[c],
            device_id={"blk": nxt}, device_id_type=MESH,
        )

    def rows(p):
        return pl.ds(pl.multiple_of(p * part, part), part)

    def send_up(k, p):
        return pltpu.make_async_remote_copy(
            src_ref=gt.at[k, rows(p)], dst_ref=from_low.at[k, rows(p)],
            send_sem=up_send.at[k, p], recv_sem=up_recv.at[k, p],
            device_id={"dp": d + 1}, device_id_type=MESH,
        )

    def send_down(k, p):
        return pltpu.make_async_remote_copy(
            src_ref=gt.at[k, rows(p)], dst_ref=from_high.at[k, rows(p)],
            send_sem=down_send.at[k, p], recv_sem=down_recv.at[k, p],
            device_id={"dp": d - 1}, device_id_type=MESH,
        )

    send_wo = pltpu.make_async_remote_copy(
        src_ref=wo_hbm, dst_ref=wo_prev, send_sem=wo_sem.at[0], recv_sem=wo_sem.at[1],
        device_id={"blk": nxt}, device_id_type=MESH,
    )
    send_att = pltpu.make_async_remote_copy(
        src_ref=att_to, dst_ref=att_from, send_sem=att_sem.at[0], recv_sem=att_sem.at[1],
        device_id={"blk": prv}, device_id_type=MESH,
    )
    odd = lax.rem(b, 2) == 1
    even = lax.rem(b, 2) == 0

    def start_out(which):
        for c in range(n):
            send_out(which, c).start()

    send_wo.start()

    @pl.when(odd)
    def _():
        start_out(0)
        start_out(1)

    def project(at, wait_x):
        def step(c, total):
            wait_x(c)
            return total + dot(xx[at, lanes(c)], w[lanes(c), :])

        return lax.fori_loop(0, n, step, jnp.zeros((count, cols), F32)).astype(BF16)

    def att_grad(weights):
        def step(c, total):
            return total + dot_nt(gg[own, lanes(c)], weights[:, lanes(c)])

        return lax.fori_loop(0, n, step, jnp.zeros((count, head), F32)).astype(BF16)

    def differentiate(slot, at, qkv, d_att_of, seg_at):
        d_qkv, attended = attention_terms(qkv, d_att_of, seg_ref[pl.ds(seg_at, 1), :], head)
        dq[slot] = d_qkv
        dt[:cols, at] = d_qkv.astype(F32).T.astype(BF16)
        dt[cols:, at] = attended.astype(F32).T.astype(BF16)

    def answer():
        send_wo.wait_recv()
        att_to[...] = att_grad(wo_prev)
        send_att.start()

    def received_att():
        send_att.wait_recv()
        return att_from[...]

    for load in loads:
        load.wait()
    differentiate(0, own, project(own, lambda c: None), lambda: att_grad(wo), b)

    @pl.when(even)
    def _():
        start_out(0)

    pl.when(odd)(answer)
    differentiate(1, far, project(far, lambda c: send_out(0, c).wait_recv()), received_att, nxt)

    def start_sums(k, first, last):
        @pl.when((d == 0) & (k > 0))
        def _():
            for p in range(first, last):
                send_up(k, p).start()

        @pl.when((d == n - 1) & (k < n - 1))
        def _():
            for p in range(first, last):
                send_down(k, p).start()

    def shard_at(i):
        return jnp.where(d == n - 1, i, n - 1 - i)

    def gradient_qkv(i, carry):
        k = shard_at(i)
        gt[k, :cols, :] = dot(dt[:cols, :], xx[:, lanes(k)]).astype(BF16)
        start_sums(k, 0, PARTS - 1)
        return carry

    lax.fori_loop(0, n, gradient_qkv, 0)
    pl.when(even)(answer)

    def far_term(c, carry):
        tsend[:, lanes(c)] = dot_nt(dq[1], w[lanes(c), :]).astype(BF16)
        send_term(c).start()
        return carry

    lax.fori_loop(0, n, far_term, 0)

    def pass_on(t, first, each):
        up, down = t - d, t - (n - 1 - d)

        @pl.when((d > 0) & (up >= 0) & (up < (n - 1 - d) * each))
        def _():
            k, p = n - 1 - up // each, first + up % each
            send_up(k, p).wait_recv()
            gt[k, rows(p), :] = (gt[k, rows(p), :].astype(F32) + from_low[k, rows(p), :].astype(F32)).astype(BF16)
            send_up(k, p).start()

        @pl.when((d < n - 1) & (down >= 0) & (down < d * each))
        def _():
            k, p = down // each, first + down % each
            send_down(k, p).wait_recv()
            gt[k, rows(p), :] = (gt[k, rows(p), :].astype(F32) + from_high[k, rows(p), :].astype(F32)).astype(BF16)
            send_down(k, p).start()

    def send_cotangent():
        for c in range(n):
            send_out(0, c).wait_send()
        pl.when(even)(lambda: start_out(1))

    ticks = 1 + (n - 2) * (PARTS - 1)
    middle = (1 + ticks) // 2
    if ticks < 2:
        send_cotangent()

    def tick_qkv(t, carry):
        pl.when(t == middle)(send_cotangent)
        pass_on(t, 0, PARTS - 1)
        return carry

    lax.fori_loop(1, ticks, tick_qkv, 0)

    def own_term(c, carry):
        term[:, lanes(c)] = dot_nt(dq[0], w[lanes(c), :])
        return carry

    lax.fori_loop(0, n, own_term, 0)

    for c in range(n):
        send_out(1, c).wait_recv()

    def gradient_out(i, carry):
        k = shard_at(i)
        gt[k, cols:, :] = dot(dt[cols:, :], gg[:, lanes(k)]).astype(BF16)
        start_sums(k, PARTS - 1, PARTS)
        return carry

    lax.fori_loop(0, n, gradient_out, 0)

    def tick_out(t, carry):
        pass_on(t, PARTS - 1, 1)
        return carry

    lax.fori_loop(1, n - 1, tick_out, 0)

    def store(c):
        return pltpu.make_async_copy(tback.at[:, lanes(c)], ig_hbm.at[:, lanes(c)], store_sem.at[c])

    def finish_input(c, carry):
        send_term(c).wait_recv()
        tback[:, lanes(c)] = (term[:, lanes(c)] + tback[:, lanes(c)].astype(F32)).astype(BF16)
        store(c).start()
        return carry

    lax.fori_loop(0, n, finish_input, 0)

    for p in range(PARTS):

        @pl.when(d == 0)
        def _(p=p):
            send_down(d, p).wait_recv()
            gs_ref[rows(p), :] = (gt[d, rows(p), :].astype(F32) + from_high[d, rows(p), :].astype(F32)).astype(BF16)

        @pl.when(d == n - 1)
        def _(p=p):
            send_up(d, p).wait_recv()
            gs_ref[rows(p), :] = (gt[d, rows(p), :].astype(F32) + from_low[d, rows(p), :].astype(F32)).astype(BF16)

        @pl.when((d > 0) & (d < n - 1))
        def _(p=p):
            send_down(d, p).wait_recv()
            send_up(d, p).wait_recv()
            gs_ref[rows(p), :] = (
                gt[d, rows(p), :].astype(F32) + from_low[d, rows(p), :].astype(F32) + from_high[d, rows(p), :].astype(F32)
            ).astype(BF16)

    send_wo.wait_send()
    send_att.wait_send()
    for c in range(n):
        send_out(1, c).wait_send()
        send_term(c).wait_send()
        store(c).wait()
        for p in range(PARTS):

            @pl.when(d < c)
            def _(c=c, p=p):
                send_up(c, p).wait_send()

            @pl.when(d > c)
            def _(c=c, p=p):
                send_down(c, p).wait_send()


def place_kernel(n, wide, ig_hbm, gs_hbm, out_ig, out_qkv, out_out, shard, turned, ig, sem):
    cols = turned.shape[1]

    def lanes(c):
        return pl.ds(c * wide, wide)

    fetch = pltpu.make_async_copy(gs_hbm, shard, sem.at[0])
    fetch.start()
    reads = [pltpu.make_async_copy(ig_hbm.at[:, lanes(c)], ig.at[:, lanes(c)], sem.at[3 + c]) for c in range(n)]
    writes = [pltpu.make_async_copy(ig.at[:, lanes(c)], out_ig.at[:, lanes(c)], sem.at[3 + n + c]) for c in range(n)]
    for read in reads:
        read.start()
    fetch.wait()
    plain = pltpu.make_async_copy(shard.at[pl.ds(cols, shard.shape[0] - cols)], out_out, sem.at[1])
    plain.start()
    for read, write in zip(reads, writes):
        read.wait()
        write.start()
    turned[...] = shard[:cols, :].astype(F32).T.astype(BF16)
    across = pltpu.make_async_copy(turned, out_qkv, sem.at[2])
    across.start()
    plain.wait()
    across.wait()
    for write in writes:
        write.wait()


def spread(array, dim, n, wide):
    shape = array.shape
    each = shape[dim] // n
    if each == wide:
        return array
    split = array.reshape(shape[:dim] + (n, each) + shape[dim + 1 :])
    pads = [(0, 0)] * split.ndim
    pads[dim + 1] = (0, wide - each)
    return jnp.pad(split, pads).reshape(shape[:dim] + (n * wide,) + shape[dim + 1 :])


def local(normed_input, segment_ids, weights_qkv, weights_out, cotangent):
    nb, n = lax.axis_size("blk"), lax.axis_size("dp")
    _, count, depth = normed_input.shape
    head = weights_out.shape[1]
    each = depth // n
    wide = -(-each // 128) * 128
    full = n * wide
    rows = 4 * head
    hbm = pl.BlockSpec(memory_space=pl.ANY)
    vmem = pl.BlockSpec(memory_space=pltpu.VMEM)
    dma = pltpu.SemaphoreType.DMA
    seq = pltpu.VMEM((count, full), BF16)
    pairs = pltpu.VMEM((2 * count, full), BF16)
    shards = pltpu.VMEM((n, rows, wide), BF16)
    input_grad, summed = pl.pallas_call(
        functools.partial(kernel, nb, n, wide),
        out_shape=(jax.ShapeDtypeStruct((count, full), BF16), jax.ShapeDtypeStruct((rows, wide), BF16)),
        in_specs=[hbm, hbm, vmem, hbm, hbm],
        out_specs=(hbm, vmem),
        scratch_shapes=[
            pairs, pairs,
            pltpu.VMEM((full, 3 * head), BF16),
            pltpu.VMEM((head, full), BF16),
            pltpu.VMEM((head, full), BF16),
            pltpu.VMEM((count, head), BF16),
            pltpu.VMEM((count, head), BF16),
            pltpu.VMEM((rows, 2 * count), BF16),
            pltpu.VMEM((2, count, 3 * head), BF16),
            shards, shards, shards,
            pltpu.VMEM((count, full), F32),
            seq, seq,
            dma((4,)), dma((2, n)), dma((2, n)), dma((2,)), dma((2,)), dma((n,)), dma((n,)),
            dma((n, PARTS)), dma((n, PARTS)), dma((n, PARTS)), dma((n, PARTS)), dma((n,)),
        ],
        compiler_params=pltpu.CompilerParams(
            collective_id=0, has_side_effects=True, vmem_limit_bytes=60 * 1024 * 1024
        ),
    )(
        spread(normed_input[0], 1, n, wide),
        spread(cotangent[0], 1, n, wide),
        segment_ids[0],
        spread(weights_qkv[0], 0, n, wide),
        spread(weights_out[0], 1, n, wide),
    )
    input_grad, grad_qkv, grad_out = pl.pallas_call(
        functools.partial(place_kernel, n, wide),
        out_shape=(
            jax.ShapeDtypeStruct((count, full), BF16),
            jax.ShapeDtypeStruct((wide, 3 * head), BF16),
            jax.ShapeDtypeStruct((head, wide), BF16),
        ),
        in_specs=[hbm, hbm],
        out_specs=(hbm, hbm, hbm),
        scratch_shapes=[
            pltpu.VMEM((rows, wide), BF16),
            pltpu.VMEM((wide, 3 * head), BF16),
            pltpu.VMEM((count, full), BF16),
            dma((3 + 2 * n,)),
        ],
        compiler_params=pltpu.CompilerParams(vmem_limit_bytes=60 * 1024 * 1024),
    )(input_grad, summed)
    if each != wide:
        input_grad = input_grad.reshape(count, n, wide)[:, :, :each].reshape(count, depth)
    return input_grad[None], grad_qkv[None, :each], grad_out[None, :, :each]


def solution(mesh):
    placed = (
        P(("blk", "dp"), None, None),
        P("dp", None, None),
        P("blk", None, None),
        P("blk", None, None),
        P(("blk", "dp"), None, None),
    )
    return jax.shard_map(
        local,
        mesh=mesh,
        in_specs=placed,
        out_specs=(P(("blk", "dp"), None, None), P("blk", "dp", None), P("blk", None, "dp")),
        check_vma=False,
    )
```

```python
import functools

import jax
import jax.numpy as jnp
from jax import lax
from jax.experimental import pallas as pl
from jax.experimental.pallas import tpu as pltpu
from jax.sharding import PartitionSpec as P

MESH = pl.DeviceIdType.MESH
F32 = jnp.float32
BF16 = jnp.bfloat16
PARTS = 4


def dot(a, b):
    return jnp.dot(a, b, preferred_element_type=F32)


def dot_nt(a, b):
    return lax.dot_general(a, b, (((1,), (1,)), ((), ())), preferred_element_type=F32)


def dot_tn(a, b):
    return lax.dot_general(a, b, (((0,), (0,)), ((), ())), preferred_element_type=F32)


def attention_terms(qkv, d_att_of, seg_row, head):
    scale = head ** (-0.5)
    query, keys, values = qkv[:, :head], qkv[:, head : 2 * head], qkv[:, 2 * head :]
    count = qkv.shape[0]
    seg_rows = jnp.broadcast_to(seg_row.astype(F32), (count, count))
    places = lax.broadcasted_iota(jnp.int32, (count, count), 0)
    others = lax.broadcasted_iota(jnp.int32, (count, count), 1)
    allowed = (places >= others) & (seg_rows.T == seg_rows)
    scores = jnp.where(allowed, dot_nt(query, keys) * scale, F32(-1e30))
    top = jnp.max(scores, axis=-1, keepdims=True)
    expo = jnp.where(allowed, jnp.exp(scores - top), F32(0.0))
    probs = expo / jnp.sum(expo, axis=-1, keepdims=True)
    probs_b = probs.astype(BF16)
    attended = dot(probs_b, values).astype(BF16)
    d_att = d_att_of()
    d_probs = dot_nt(d_att, values)
    d_scores = (probs * (d_probs - jnp.sum(probs * d_probs, axis=-1, keepdims=True)) * scale).astype(BF16)
    d_qkv = jnp.concatenate([dot(d_scores, keys), dot_tn(d_scores, query), dot_tn(probs_b, d_att)], axis=1)
    return d_qkv.astype(BF16), attended


def kernel(
    nb, n, wide, x_hbm, g_hbm, seg_ref, w_hbm, wo_hbm, ig_hbm, turned, plain,
    xx, gg, w, wo, dt, dq, gt, from_low, from_high, term, tsend, tback,
    load_sem, out_send, out_recv, t_send, t_recv, up_send, up_recv, down_send, down_recv, store_sem,
):
    b, d = lax.axis_index("blk"), lax.axis_index("dp")
    nxt, prv = lax.rem(b + 1, nb), lax.rem(b + nb - 1, nb)
    head = wo.shape[0]
    cols = 3 * head
    count = tsend.shape[0]
    part = head
    own, far = pl.ds(0, count), pl.ds(count, count)

    loads = [
        pltpu.make_async_copy(src, dst, load_sem.at[i])
        for i, (src, dst) in enumerate(((x_hbm, xx.at[own]), (w_hbm, w), (g_hbm, gg.at[own]), (wo_hbm, wo)))
    ]
    for load in loads:
        load.start()

    barrier = pltpu.get_barrier_semaphore()
    for other in (nxt, prv):
        pl.semaphore_signal(barrier, inc=1, device_id={"blk": other}, device_id_type=MESH)

    @pl.when(d > 0)
    def _():
        pl.semaphore_signal(barrier, inc=1, device_id={"dp": d - 1}, device_id_type=MESH)

    @pl.when(d < n - 1)
    def _():
        pl.semaphore_signal(barrier, inc=1, device_id={"dp": d + 1}, device_id_type=MESH)

    pl.semaphore_wait(barrier, 2 + (d > 0).astype(jnp.int32) + (d < n - 1).astype(jnp.int32))

    def lanes(c):
        return pl.ds(pl.multiple_of(c * wide, 128), wide)

    def send_out(which, c):
        src, dst = ((x_hbm, xx), (g_hbm, gg))[which]
        return pltpu.make_async_remote_copy(
            src_ref=src.at[:, lanes(c)], dst_ref=dst.at[far, lanes(c)],
            send_sem=out_send.at[which, c], recv_sem=out_recv.at[which, c],
            device_id={"blk": prv}, device_id_type=MESH,
        )

    def send_term(c):
        return pltpu.make_async_remote_copy(
            src_ref=tsend.at[:, lanes(c)], dst_ref=tback.at[:, lanes(c)],
            send_sem=t_send.at[c], recv_sem=t_recv.at[c],
            device_id={"blk": nxt}, device_id_type=MESH,
        )

    def rows(p):
        return pl.ds(pl.multiple_of(p * part, part), part)

    def send_up(k, p):
        return pltpu.make_async_remote_copy(
            src_ref=gt.at[k, rows(p)], dst_ref=from_low.at[k, rows(p)],
            send_sem=up_send.at[k, p], recv_sem=up_recv.at[k, p],
            device_id={"dp": d + 1}, device_id_type=MESH,
        )

    def send_down(k, p):
        return pltpu.make_async_remote_copy(
            src_ref=gt.at[k, rows(p)], dst_ref=from_high.at[k, rows(p)],
            send_sem=down_send.at[k, p], recv_sem=down_recv.at[k, p],
            device_id={"dp": d - 1}, device_id_type=MESH,
        )

    for which in range(2):
        for c in range(n):
            send_out(which, c).start()

    def differentiate(slot, at, wait_x, wait_g, seg_at):
        def qkv_step(c, total):
            wait_x(c)
            return total + dot(xx[at, lanes(c)], w[lanes(c), :])

        def att_step(c, total):
            wait_g(c)
            return total + dot_nt(gg[at, lanes(c)], wo[:, lanes(c)])

        qkv = lax.fori_loop(0, n, qkv_step, jnp.zeros((count, cols), F32)).astype(BF16)

        def d_att_of():
            return lax.fori_loop(0, n, att_step, jnp.zeros((count, head), F32)).astype(BF16)

        d_qkv, attended = attention_terms(qkv, d_att_of, seg_ref[pl.ds(seg_at, 1), :], head)
        dq[slot] = d_qkv
        dt[:cols, at] = d_qkv.astype(F32).T.astype(BF16)
        dt[cols:, at] = attended.astype(F32).T.astype(BF16)

    for load in loads:
        load.wait()
    differentiate(0, own, lambda c: None, lambda c: None, b)

    differentiate(1, far, lambda c: send_out(0, c).wait_recv(), lambda c: send_out(1, c).wait_recv(), nxt)

    def gradient(i, carry):
        k = jnp.where(d == n - 1, i, n - 1 - i)
        gt[k, :cols, :] = dot(dt[:cols, :], xx[:, lanes(k)]).astype(BF16)
        gt[k, cols:, :] = dot(dt[cols:, :], gg[:, lanes(k)]).astype(BF16)

        @pl.when((d == 0) & (k > 0))
        def _():
            for p in range(PARTS):
                send_up(k, p).start()

        @pl.when((d == n - 1) & (k < n - 1))
        def _():
            for p in range(PARTS):
                send_down(k, p).start()

        return carry

    lax.fori_loop(0, n, gradient, 0)

    def far_term(c, carry):
        tsend[:, lanes(c)] = dot_nt(dq[1], w[lanes(c), :]).astype(BF16)
        send_term(c).start()
        return carry

    lax.fori_loop(0, n, far_term, 0)

    def tick(t, carry):
        up, down = t - d, t - (n - 1 - d)

        @pl.when((d > 0) & (up >= 0) & (up < (n - 1 - d) * PARTS))
        def _():
            k, p = n - 1 - up // PARTS, up % PARTS
            send_up(k, p).wait_recv()
            gt[k, rows(p), :] = (gt[k, rows(p), :].astype(F32) + from_low[k, rows(p), :].astype(F32)).astype(BF16)
            send_up(k, p).start()

        @pl.when((d < n - 1) & (down >= 0) & (down < d * PARTS))
        def _():
            k, p = down // PARTS, down % PARTS
            send_down(k, p).wait_recv()
            gt[k, rows(p), :] = (gt[k, rows(p), :].astype(F32) + from_high[k, rows(p), :].astype(F32)).astype(BF16)
            send_down(k, p).start()

        return carry

    lax.fori_loop(1, 1 + (n - 2) * PARTS, tick, 0)

    def own_term(c, carry):
        term[:, lanes(c)] = dot_nt(dq[0], w[lanes(c), :])
        return carry

    lax.fori_loop(0, n, own_term, 0)

    def store(c):
        return pltpu.make_async_copy(tback.at[:, lanes(c)], ig_hbm.at[:, lanes(c)], store_sem.at[c])

    def finish_input(c, carry):
        send_term(c).wait_recv()
        tback[:, lanes(c)] = (term[:, lanes(c)] + tback[:, lanes(c)].astype(F32)).astype(BF16)
        store(c).start()
        return carry

    lax.fori_loop(0, n, finish_input, 0)

    for p in range(PARTS):
        pl.when(d > 0)(lambda p=p: send_up(d, p).wait_recv())
        pl.when(d < n - 1)(lambda p=p: send_down(d, p).wait_recv())
        total = gt[d, rows(p), :].astype(F32)
        total += jnp.where(d > 0, from_low[d, rows(p), :].astype(F32), F32(0.0))
        total += jnp.where(d < n - 1, from_high[d, rows(p), :].astype(F32), F32(0.0))
        if p < PARTS - 1:
            turned[:, rows(p)] = total.T.astype(BF16)
        else:
            plain[...] = total.astype(BF16)

    for c in range(n):
        send_out(0, c).wait_send()
        send_out(1, c).wait_send()
        send_term(c).wait_send()
        store(c).wait()
        for p in range(PARTS):

            @pl.when(d < c)
            def _(c=c, p=p):
                send_up(c, p).wait_send()

            @pl.when(d > c)
            def _(c=c, p=p):
                send_down(c, p).wait_send()


def place_kernel(n, wide, ig_hbm, qkv_hbm, out_hbm, ig_to, qkv_to, out_to, ig, qkv, out, sem):
    def lanes(c):
        return pl.ds(c * wide, wide)

    legs = [(ig_hbm.at[:, lanes(c)], ig.at[:, lanes(c)], ig_to.at[:, lanes(c)]) for c in range(n)]
    legs += [(qkv_hbm, qkv, qkv_to), (out_hbm, out, out_to)]
    reads = [pltpu.make_async_copy(src, mid, sem.at[0, i]) for i, (src, mid, _) in enumerate(legs)]
    writes = [pltpu.make_async_copy(mid, dst, sem.at[1, i]) for i, (_, mid, dst) in enumerate(legs)]
    for read in reads:
        read.start()
    for read, write in zip(reads, writes):
        read.wait()
        write.start()
    for write in writes:
        write.wait()


def spread(array, dim, n, wide):
    shape = array.shape
    each = shape[dim] // n
    if each == wide:
        return array
    split = array.reshape(shape[:dim] + (n, each) + shape[dim + 1 :])
    pads = [(0, 0)] * split.ndim
    pads[dim + 1] = (0, wide - each)
    return jnp.pad(split, pads).reshape(shape[:dim] + (n * wide,) + shape[dim + 1 :])


def local(normed_input, segment_ids, weights_qkv, weights_out, cotangent):
    nb, n = lax.axis_size("blk"), lax.axis_size("dp")
    _, count, depth = normed_input.shape
    head = weights_out.shape[1]
    each = depth // n
    wide = -(-each // 128) * 128
    full = n * wide
    rows = 4 * head
    hbm = pl.BlockSpec(memory_space=pl.ANY)
    vmem = pl.BlockSpec(memory_space=pltpu.VMEM)
    dma = pltpu.SemaphoreType.DMA
    seq = pltpu.VMEM((count, full), BF16)
    pairs = pltpu.VMEM((2 * count, full), BF16)
    shards = pltpu.VMEM((n, rows, wide), BF16)
    results = (
        jax.ShapeDtypeStruct((count, full), BF16),
        jax.ShapeDtypeStruct((wide, 3 * head), BF16),
        jax.ShapeDtypeStruct((head, wide), BF16),
    )
    made = pl.pallas_call(
        functools.partial(kernel, nb, n, wide),
        out_shape=results,
        in_specs=[hbm, hbm, vmem, hbm, hbm],
        out_specs=(hbm, vmem, vmem),
        scratch_shapes=[
            pairs, pairs,
            pltpu.VMEM((full, 3 * head), BF16),
            pltpu.VMEM((head, full), BF16),
            pltpu.VMEM((rows, 2 * count), BF16),
            pltpu.VMEM((2, count, 3 * head), BF16),
            shards, shards, shards,
            pltpu.VMEM((count, full), F32),
            seq, seq,
            dma((4,)), dma((2, n)), dma((2, n)), dma((n,)), dma((n,)),
            dma((n, PARTS)), dma((n, PARTS)), dma((n, PARTS)), dma((n, PARTS)), dma((n,)),
        ],
        compiler_params=pltpu.CompilerParams(
            collective_id=0, has_side_effects=True, vmem_limit_bytes=60 * 1024 * 1024
        ),
    )(
        spread(normed_input[0], 1, n, wide),
        spread(cotangent[0], 1, n, wide),
        segment_ids[0],
        spread(weights_qkv[0], 0, n, wide),
        spread(weights_out[0], 1, n, wide),
    )
    input_grad, grad_qkv, grad_out = pl.pallas_call(
        functools.partial(place_kernel, n, wide),
        out_shape=results,
        in_specs=[hbm, hbm, hbm],
        out_specs=(hbm, hbm, hbm),
        scratch_shapes=[pltpu.VMEM(made_one.shape, BF16) for made_one in results] + [dma((2, n + 2))],
        compiler_params=pltpu.CompilerParams(vmem_limit_bytes=60 * 1024 * 1024),
    )(*made)
    if each != wide:
        input_grad = input_grad.reshape(count, n, wide)[:, :, :each].reshape(count, depth)
    return input_grad[None], grad_qkv[None, :each], grad_out[None, :, :each]


def solution(mesh):
    placed = (
        P(("blk", "dp"), None, None),
        P("dp", None, None),
        P("blk", None, None),
        P("blk", None, None),
        P(("blk", "dp"), None, None),
    )
    return jax.shard_map(
        local,
        mesh=mesh,
        in_specs=placed,
        out_specs=(P(("blk", "dp"), None, None), P("blk", "dp", None), P("blk", None, "dp")),
        check_vma=False,
    )
```

```python
import functools

import jax
import jax.numpy as jnp
from jax import lax
from jax.experimental import pallas as pl
from jax.experimental.pallas import tpu as pltpu
from jax.sharding import PartitionSpec as P

MESH = pl.DeviceIdType.MESH
F32 = jnp.float32
BF16 = jnp.bfloat16
PARTS = 4


def dot(a, b):
    return jnp.dot(a, b, preferred_element_type=F32)


def dot_nt(a, b):
    return lax.dot_general(a, b, (((1,), (1,)), ((), ())), preferred_element_type=F32)


def dot_tn(a, b):
    return lax.dot_general(a, b, (((0,), (0,)), ((), ())), preferred_element_type=F32)


def attention_terms(qkv, d_att_of, seg_row, head):
    scale = head ** (-0.5)
    query, keys, values = qkv[:, :head], qkv[:, head : 2 * head], qkv[:, 2 * head :]
    count = qkv.shape[0]
    seg_rows = jnp.broadcast_to(seg_row.astype(F32), (count, count))
    places = lax.broadcasted_iota(jnp.int32, (count, count), 0)
    others = lax.broadcasted_iota(jnp.int32, (count, count), 1)
    allowed = (places >= others) & (seg_rows.T == seg_rows)
    scores = jnp.where(allowed, dot_nt(query, keys) * scale, F32(-1e30))
    top = jnp.max(scores, axis=-1, keepdims=True)
    expo = jnp.where(allowed, jnp.exp(scores - top), F32(0.0))
    probs = expo / jnp.sum(expo, axis=-1, keepdims=True)
    probs_b = probs.astype(BF16)
    attended = dot(probs_b, values).astype(BF16)
    d_att = d_att_of()
    d_probs = dot_nt(d_att, values)
    d_scores = (probs * (d_probs - jnp.sum(probs * d_probs, axis=-1, keepdims=True)) * scale).astype(BF16)
    d_qkv = jnp.concatenate([dot(d_scores, keys), dot_tn(d_scores, query), dot_tn(probs_b, d_att)], axis=1)
    return d_qkv.astype(BF16), attended


def kernel(
    nb, n, wide, x_hbm, g_hbm, seg_ref, w_hbm, wo_hbm, ig_hbm, turned, plain,
    xx, gg, w, wo, wo_prev, go_to, go_from, att_to, att_from, back_to, back_from, turned_att, dt, dq, gt, from_low, from_high, term, tsend, tback,
    load_sem, x_send, x_recv, go_send, go_recv, wo_sem, att_sem, back_sem, t_send, t_recv, up_send, up_recv, down_send, down_recv, store_sem,
):
    b, d = lax.axis_index("blk"), lax.axis_index("dp")
    nxt, prv = lax.rem(b + 1, nb), lax.rem(b + nb - 1, nb)
    head = wo.shape[0]
    cols = 3 * head
    count = tsend.shape[0]
    part = head
    own, far = pl.ds(0, count), pl.ds(count, count)

    loads = [
        pltpu.make_async_copy(src, dst, load_sem.at[i])
        for i, (src, dst) in enumerate(((x_hbm, xx.at[own]), (w_hbm, w), (g_hbm, gg), (wo_hbm, wo)))
    ]
    for load in loads:
        load.start()

    barrier = pltpu.get_barrier_semaphore()
    for other in (nxt, prv):
        pl.semaphore_signal(barrier, inc=1, device_id={"blk": other}, device_id_type=MESH)

    @pl.when(d > 0)
    def _():
        pl.semaphore_signal(barrier, inc=1, device_id={"dp": d - 1}, device_id_type=MESH)

    @pl.when(d < n - 1)
    def _():
        pl.semaphore_signal(barrier, inc=1, device_id={"dp": d + 1}, device_id_type=MESH)

    pl.semaphore_wait(barrier, 2 + (d > 0).astype(jnp.int32) + (d < n - 1).astype(jnp.int32))

    def lanes(c):
        return pl.ds(pl.multiple_of(c * wide, 128), wide)

    def send_x(c):
        return pltpu.make_async_remote_copy(
            src_ref=x_hbm.at[:, lanes(c)], dst_ref=xx.at[far, lanes(c)],
            send_sem=x_send.at[c], recv_sem=x_recv.at[c],
            device_id={"blk": prv}, device_id_type=MESH,
        )

    def send_go(c):
        return pltpu.make_async_remote_copy(
            src_ref=go_to.at[:, lanes(c)], dst_ref=go_from.at[:, lanes(c)],
            send_sem=go_send.at[c], recv_sem=go_recv.at[c],
            device_id={"blk": prv}, device_id_type=MESH,
        )

    def send_term(c):
        return pltpu.make_async_remote_copy(
            src_ref=tsend.at[:, lanes(c)], dst_ref=tback.at[:, lanes(c)],
            send_sem=t_send.at[c], recv_sem=t_recv.at[c],
            device_id={"blk": nxt}, device_id_type=MESH,
        )

    def rows(p):
        return pl.ds(pl.multiple_of(p * part, part), part)

    def send_up(k, p):
        return pltpu.make_async_remote_copy(
            src_ref=gt.at[k, rows(p)], dst_ref=from_low.at[k, rows(p)],
            send_sem=up_send.at[k, p], recv_sem=up_recv.at[k, p],
            device_id={"dp": d + 1}, device_id_type=MESH,
        )

    def send_down(k, p):
        return pltpu.make_async_remote_copy(
            src_ref=gt.at[k, rows(p)], dst_ref=from_high.at[k, rows(p)],
            send_sem=down_send.at[k, p], recv_sem=down_recv.at[k, p],
            device_id={"dp": d - 1}, device_id_type=MESH,
        )

    send_wo = pltpu.make_async_remote_copy(
        src_ref=wo_hbm, dst_ref=wo_prev, send_sem=wo_sem.at[0], recv_sem=wo_sem.at[1],
        device_id={"blk": nxt}, device_id_type=MESH,
    )
    send_att = pltpu.make_async_remote_copy(
        src_ref=att_to, dst_ref=att_from, send_sem=att_sem.at[0], recv_sem=att_sem.at[1],
        device_id={"blk": prv}, device_id_type=MESH,
    )
    send_back = pltpu.make_async_remote_copy(
        src_ref=back_to, dst_ref=back_from, send_sem=back_sem.at[0], recv_sem=back_sem.at[1],
        device_id={"blk": nxt}, device_id_type=MESH,
    )
    odd = lax.rem(b, 2) == 1
    even = lax.rem(b, 2) == 0

    def start_x():
        for c in range(n):
            send_x(c).start()

    send_wo.start()

    pl.when(odd)(start_x)

    def project(at, wait_x):
        def step(c, total):
            wait_x(c)
            return total + dot(xx[at, lanes(c)], w[lanes(c), :])

        return lax.fori_loop(0, n, step, jnp.zeros((count, cols), F32)).astype(BF16)

    def att_grad(weights):
        def step(c, total):
            return total + dot_nt(gg[:, lanes(c)], weights[:, lanes(c)])

        return lax.fori_loop(0, n, step, jnp.zeros((count, head), F32)).astype(BF16)

    def differentiate(slot, at, qkv, d_att_of, seg_at):
        d_qkv, attended = attention_terms(qkv, d_att_of, seg_ref[pl.ds(seg_at, 1), :], head)
        dq[slot] = d_qkv
        dt[:, at] = d_qkv.astype(F32).T.astype(BF16)
        return attended.astype(F32).T.astype(BF16)

    def answer():
        send_wo.wait_recv()
        att_to[...] = att_grad(wo_prev)
        send_att.start()

    def received_att():
        send_att.wait_recv()
        return att_from[...]

    for load in loads:
        load.wait()
    pl.when(odd)(answer)
    turned_att[...] = differentiate(0, own, project(own, lambda c: None), lambda: att_grad(wo), b)

    pl.when(even)(start_x)

    def shard_at(i):
        return jnp.where(d == n - 1, i, n - 1 - i)

    def out_gradient_back():
        send_back.wait_recv()

        def step(i, carry):
            k = shard_at(i)
            go_to[:, lanes(k)] = dot(back_from[...], gg[:, lanes(k)]).astype(BF16)
            send_go(k).start()
            return carry

        lax.fori_loop(0, n, step, 0)

    pl.when(odd)(out_gradient_back)

    back_to[...] = differentiate(1, far, project(far, lambda c: send_x(c).wait_recv()), received_att, nxt)
    send_back.start()

    def start_sums(k, first, last):
        @pl.when((d == 0) & (k > 0))
        def _():
            for p in range(first, last):
                send_up(k, p).start()

        @pl.when((d == n - 1) & (k < n - 1))
        def _():
            for p in range(first, last):
                send_down(k, p).start()

    def gradient_qkv(i, carry):
        k = shard_at(i)
        gt[k, :cols, :] = dot(dt[...], xx[:, lanes(k)]).astype(BF16)
        start_sums(k, 0, PARTS - 1)
        return carry

    lax.fori_loop(0, n, gradient_qkv, 0)
    pl.when(even)(answer)

    def far_term(c, carry):
        tsend[:, lanes(c)] = dot_nt(dq[1], w[lanes(c), :]).astype(BF16)
        send_term(c).start()
        return carry

    lax.fori_loop(0, n, far_term, 0)

    def pass_on(t, first, each):
        up, down = t - d, t - (n - 1 - d)

        @pl.when((d > 0) & (up >= 0) & (up < (n - 1 - d) * each))
        def _():
            k, p = n - 1 - up // each, first + up % each
            send_up(k, p).wait_recv()
            gt[k, rows(p), :] = (gt[k, rows(p), :].astype(F32) + from_low[k, rows(p), :].astype(F32)).astype(BF16)
            send_up(k, p).start()

        @pl.when((d < n - 1) & (down >= 0) & (down < d * each))
        def _():
            k, p = down // each, first + down % each
            send_down(k, p).wait_recv()
            gt[k, rows(p), :] = (gt[k, rows(p), :].astype(F32) + from_high[k, rows(p), :].astype(F32)).astype(BF16)
            send_down(k, p).start()

    ticks = 1 + (n - 2) * (PARTS - 1)

    def tick_qkv(t, carry):
        pass_on(t, 0, PARTS - 1)
        return carry

    lax.fori_loop(1, ticks, tick_qkv, 0)

    def own_term(c, carry):
        term[:, lanes(c)] = dot_nt(dq[0], w[lanes(c), :])
        return carry

    lax.fori_loop(0, n, own_term, 0)

    pl.when(even)(out_gradient_back)

    def gradient_out(i, carry):
        k = shard_at(i)
        send_go(k).wait_recv()
        gt[k, cols:, :] = (dot(turned_att[...], gg[:, lanes(k)]) + go_from[:, lanes(k)].astype(F32)).astype(BF16)
        start_sums(k, PARTS - 1, PARTS)
        return carry

    lax.fori_loop(0, n, gradient_out, 0)

    def tick_out(t, carry):
        pass_on(t, PARTS - 1, 1)
        return carry

    lax.fori_loop(1, n - 1, tick_out, 0)

    def store(c):
        return pltpu.make_async_copy(tback.at[:, lanes(c)], ig_hbm.at[:, lanes(c)], store_sem.at[c])

    def finish_input(c, carry):
        send_term(c).wait_recv()
        tback[:, lanes(c)] = (term[:, lanes(c)] + tback[:, lanes(c)].astype(F32)).astype(BF16)
        store(c).start()
        return carry

    lax.fori_loop(0, n, finish_input, 0)

    for p in range(PARTS):
        pl.when(d > 0)(lambda p=p: send_up(d, p).wait_recv())
        pl.when(d < n - 1)(lambda p=p: send_down(d, p).wait_recv())
        total = gt[d, rows(p), :].astype(F32)
        total += jnp.where(d > 0, from_low[d, rows(p), :].astype(F32), F32(0.0))
        total += jnp.where(d < n - 1, from_high[d, rows(p), :].astype(F32), F32(0.0))
        if p < PARTS - 1:
            turned[:, rows(p)] = total.T.astype(BF16)
        else:
            plain[...] = total.astype(BF16)

    send_wo.wait_send()
    send_att.wait_send()
    send_back.wait_send()
    for c in range(n):
        send_x(c).wait_send()
        send_go(c).wait_send()
        send_term(c).wait_send()
        store(c).wait()
        for p in range(PARTS):

            @pl.when(d < c)
            def _(c=c, p=p):
                send_up(c, p).wait_send()

            @pl.when(d > c)
            def _(c=c, p=p):
                send_down(c, p).wait_send()


def place_kernel(n, wide, ig_hbm, qkv_hbm, out_hbm, ig_to, qkv_to, out_to, ig, qkv, out, sem):
    def lanes(c):
        return pl.ds(c * wide, wide)

    legs = [(ig_hbm.at[:, lanes(c)], ig.at[:, lanes(c)], ig_to.at[:, lanes(c)]) for c in range(n)]
    legs += [(qkv_hbm, qkv, qkv_to), (out_hbm, out, out_to)]
    reads = [pltpu.make_async_copy(src, mid, sem.at[0, i]) for i, (src, mid, _) in enumerate(legs)]
    writes = [pltpu.make_async_copy(mid, dst, sem.at[1, i]) for i, (_, mid, dst) in enumerate(legs)]
    for read in reads:
        read.start()
    for read, write in zip(reads, writes):
        read.wait()
        write.start()
    for write in writes:
        write.wait()


def spread(array, dim, n, wide):
    shape = array.shape
    each = shape[dim] // n
    if each == wide:
        return array
    split = array.reshape(shape[:dim] + (n, each) + shape[dim + 1 :])
    pads = [(0, 0)] * split.ndim
    pads[dim + 1] = (0, wide - each)
    return jnp.pad(split, pads).reshape(shape[:dim] + (n * wide,) + shape[dim + 1 :])


def local(normed_input, segment_ids, weights_qkv, weights_out, cotangent):
    nb, n = lax.axis_size("blk"), lax.axis_size("dp")
    _, count, depth = normed_input.shape
    head = weights_out.shape[1]
    each = depth // n
    wide = -(-each // 128) * 128
    full = n * wide
    rows = 4 * head
    hbm = pl.BlockSpec(memory_space=pl.ANY)
    vmem = pl.BlockSpec(memory_space=pltpu.VMEM)
    dma = pltpu.SemaphoreType.DMA
    seq = pltpu.VMEM((count, full), BF16)
    pairs = pltpu.VMEM((2 * count, full), BF16)
    heads = pltpu.VMEM((head, full), BF16)
    shards = pltpu.VMEM((n, rows, wide), BF16)
    results = (
        jax.ShapeDtypeStruct((count, full), BF16),
        jax.ShapeDtypeStruct((wide, 3 * head), BF16),
        jax.ShapeDtypeStruct((head, wide), BF16),
    )
    made = pl.pallas_call(
        functools.partial(kernel, nb, n, wide),
        out_shape=results,
        in_specs=[hbm, hbm, vmem, hbm, hbm],
        out_specs=(hbm, vmem, vmem),
        scratch_shapes=[
            pairs, seq,
            pltpu.VMEM((full, 3 * head), BF16),
            heads, heads, heads, heads,
            pltpu.VMEM((count, head), BF16),
            pltpu.VMEM((count, head), BF16),
            pltpu.VMEM((head, count), BF16),
            pltpu.VMEM((head, count), BF16),
            pltpu.VMEM((head, count), BF16),
            pltpu.VMEM((3 * head, 2 * count), BF16),
            pltpu.VMEM((2, count, 3 * head), BF16),
            shards, shards, shards,
            pltpu.VMEM((count, full), F32),
            seq, seq,
            dma((4,)), dma((n,)), dma((n,)), dma((n,)), dma((n,)), dma((2,)), dma((2,)), dma((2,)), dma((n,)), dma((n,)),
            dma((n, PARTS)), dma((n, PARTS)), dma((n, PARTS)), dma((n, PARTS)), dma((n,)),
        ],
        compiler_params=pltpu.CompilerParams(
            collective_id=0, has_side_effects=True, vmem_limit_bytes=60 * 1024 * 1024
        ),
    )(
        spread(normed_input[0], 1, n, wide),
        spread(cotangent[0], 1, n, wide),
        segment_ids[0],
        spread(weights_qkv[0], 0, n, wide),
        spread(weights_out[0], 1, n, wide),
    )
    input_grad, grad_qkv, grad_out = pl.pallas_call(
        functools.partial(place_kernel, n, wide),
        out_shape=results,
        in_specs=[hbm, hbm, hbm],
        out_specs=(hbm, hbm, hbm),
        scratch_shapes=[pltpu.VMEM(made_one.shape, BF16) for made_one in results] + [dma((2, n + 2))],
        compiler_params=pltpu.CompilerParams(vmem_limit_bytes=60 * 1024 * 1024),
    )(*made)
    if each != wide:
        input_grad = input_grad.reshape(count, n, wide)[:, :, :each].reshape(count, depth)
    return input_grad[None], grad_qkv[None, :each], grad_out[None, :, :each]


def solution(mesh):
    placed = (
        P(("blk", "dp"), None, None),
        P("dp", None, None),
        P("blk", None, None),
        P("blk", None, None),
        P(("blk", "dp"), None, None),
    )
    return jax.shard_map(
        local,
        mesh=mesh,
        in_specs=placed,
        out_specs=(P(("blk", "dp"), None, None), P("blk", "dp", None), P("blk", None, "dp")),
        check_vma=False,
    )
```

```python
import functools

import jax
import jax.numpy as jnp
from jax import lax
from jax.experimental import pallas as pl
from jax.experimental.pallas import tpu as pltpu
from jax.sharding import PartitionSpec as P

MESH = pl.DeviceIdType.MESH
F32 = jnp.float32
BF16 = jnp.bfloat16
PARTS = 4


def dot(a, b):
    return jnp.dot(a, b, preferred_element_type=F32)


def dot_nt(a, b):
    return lax.dot_general(a, b, (((1,), (1,)), ((), ())), preferred_element_type=F32)


def dot_tn(a, b):
    return lax.dot_general(a, b, (((0,), (0,)), ((), ())), preferred_element_type=F32)


def attention_terms(qkv, d_att_of, seg_row, head):
    scale = head ** (-0.5)
    query, keys, values = qkv[:, :head], qkv[:, head : 2 * head], qkv[:, 2 * head :]
    count = qkv.shape[0]
    seg_rows = jnp.broadcast_to(seg_row.astype(F32), (count, count))
    places = lax.broadcasted_iota(jnp.int32, (count, count), 0)
    others = lax.broadcasted_iota(jnp.int32, (count, count), 1)
    allowed = (places >= others) & (seg_rows.T == seg_rows)
    scores = jnp.where(allowed, dot_nt(query, keys) * scale, F32(-1e30))
    top = jnp.max(scores, axis=-1, keepdims=True)
    expo = jnp.where(allowed, jnp.exp(scores - top), F32(0.0))
    probs = expo / jnp.sum(expo, axis=-1, keepdims=True)
    probs_b = probs.astype(BF16)
    attended = dot(probs_b, values).astype(BF16)
    d_att = d_att_of()
    d_probs = dot_nt(d_att, values)
    d_scores = (probs * (d_probs - jnp.sum(probs * d_probs, axis=-1, keepdims=True)) * scale).astype(BF16)
    d_qkv = jnp.concatenate([dot(d_scores, keys), dot_tn(d_scores, query), dot_tn(probs_b, d_att)], axis=1)
    return d_qkv.astype(BF16), attended


def kernel(
    nb, n, wide, x_hbm, g_hbm, seg_ref, w_hbm, wo_hbm, ig_hbm, turned, plain,
    xx, gg, w, wo, wo_prev, go_to, go_from, att_to, att_from, back_to, back_from, turned_att, dt, dq, gt, from_low, from_high, term, tsend, tback,
    load_sem, x_send, x_recv, go_send, go_recv, wo_sem, att_sem, back_sem, t_send, t_recv, up_send, up_recv, down_send, down_recv, store_sem,
):
    b, d = lax.axis_index("blk"), lax.axis_index("dp")
    nxt, prv = lax.rem(b + 1, nb), lax.rem(b + nb - 1, nb)
    head = wo.shape[0]
    cols = 3 * head
    count = tsend.shape[0]
    part = head
    own, far = pl.ds(0, count), pl.ds(count, count)

    loads = [
        pltpu.make_async_copy(src, dst, load_sem.at[i])
        for i, (src, dst) in enumerate(((x_hbm, xx.at[own]), (w_hbm, w), (g_hbm, gg), (wo_hbm, wo)))
    ]
    for load in loads:
        load.start()

    barrier = pltpu.get_barrier_semaphore()
    for other in (nxt, prv):
        pl.semaphore_signal(barrier, inc=1, device_id={"blk": other}, device_id_type=MESH)

    @pl.when(d > 0)
    def _():
        pl.semaphore_signal(barrier, inc=1, device_id={"dp": d - 1}, device_id_type=MESH)

    @pl.when(d < n - 1)
    def _():
        pl.semaphore_signal(barrier, inc=1, device_id={"dp": d + 1}, device_id_type=MESH)

    pl.semaphore_wait(barrier, 2 + (d > 0).astype(jnp.int32) + (d < n - 1).astype(jnp.int32))

    def lanes(c):
        return pl.ds(pl.multiple_of(c * wide, 128), wide)

    def send_x(c):
        return pltpu.make_async_remote_copy(
            src_ref=x_hbm.at[:, lanes(c)], dst_ref=xx.at[far, lanes(c)],
            send_sem=x_send.at[c], recv_sem=x_recv.at[c],
            device_id={"blk": prv}, device_id_type=MESH,
        )

    def send_go(c):
        return pltpu.make_async_remote_copy(
            src_ref=go_to.at[:, lanes(c)], dst_ref=go_from.at[:, lanes(c)],
            send_sem=go_send.at[c], recv_sem=go_recv.at[c],
            device_id={"blk": prv}, device_id_type=MESH,
        )

    def send_term(c):
        return pltpu.make_async_remote_copy(
            src_ref=tsend.at[:, lanes(c)], dst_ref=tback.at[:, lanes(c)],
            send_sem=t_send.at[c], recv_sem=t_recv.at[c],
            device_id={"blk": nxt}, device_id_type=MESH,
        )

    def rows(p):
        return pl.ds(pl.multiple_of(p * part, part), part)

    def send_up(k, p):
        return pltpu.make_async_remote_copy(
            src_ref=gt.at[k, rows(p)], dst_ref=from_low.at[k, rows(p)],
            send_sem=up_send.at[k, p], recv_sem=up_recv.at[k, p],
            device_id={"dp": d + 1}, device_id_type=MESH,
        )

    def send_down(k, p):
        return pltpu.make_async_remote_copy(
            src_ref=gt.at[k, rows(p)], dst_ref=from_high.at[k, rows(p)],
            send_sem=down_send.at[k, p], recv_sem=down_recv.at[k, p],
            device_id={"dp": d - 1}, device_id_type=MESH,
        )

    send_wo = pltpu.make_async_remote_copy(
        src_ref=wo_hbm, dst_ref=wo_prev, send_sem=wo_sem.at[0], recv_sem=wo_sem.at[1],
        device_id={"blk": nxt}, device_id_type=MESH,
    )
    send_att = pltpu.make_async_remote_copy(
        src_ref=att_to, dst_ref=att_from, send_sem=att_sem.at[0], recv_sem=att_sem.at[1],
        device_id={"blk": prv}, device_id_type=MESH,
    )
    send_back = pltpu.make_async_remote_copy(
        src_ref=back_to, dst_ref=back_from, send_sem=back_sem.at[0], recv_sem=back_sem.at[1],
        device_id={"blk": nxt}, device_id_type=MESH,
    )
    odd = lax.rem(b, 2) == 1
    even = lax.rem(b, 2) == 0

    def start_x():
        for c in range(n):
            send_x(c).start()

    send_wo.start()

    pl.when(odd)(start_x)

    def project(at, wait_x):
        def step(c, total):
            wait_x(c)
            return total + dot(xx[at, lanes(c)], w[lanes(c), :])

        return lax.fori_loop(0, n, step, jnp.zeros((count, cols), F32)).astype(BF16)

    def att_grad(weights):
        def step(c, total):
            return total + dot_nt(gg[:, lanes(c)], weights[:, lanes(c)])

        return lax.fori_loop(0, n, step, jnp.zeros((count, head), F32)).astype(BF16)

    def differentiate(slot, at, qkv, d_att_of, seg_at):
        d_qkv, attended = attention_terms(qkv, d_att_of, seg_ref[pl.ds(seg_at, 1), :], head)
        dq[slot] = d_qkv
        dt[:, at] = d_qkv.astype(F32).T.astype(BF16)
        return attended.astype(F32).T.astype(BF16)

    def answer():
        send_wo.wait_recv()
        att_to[...] = att_grad(wo_prev)
        send_att.start()

    def received_att():
        send_att.wait_recv()
        return att_from[...]

    for load in loads:
        load.wait()
    pl.when(odd)(answer)
    turned_att[...] = differentiate(0, own, project(own, lambda c: None), lambda: att_grad(wo), b)

    pl.when(even)(start_x)

    def shard_at(i):
        return jnp.where(d == n - 1, i, n - 1 - i)

    def out_gradient_back():
        send_back.wait_recv()

        def step(i, carry):
            k = shard_at(i)
            go_to[:, lanes(k)] = dot(back_from[...], gg[:, lanes(k)]).astype(BF16)
            send_go(k).start()
            return carry

        lax.fori_loop(0, n, step, 0)

    pl.when(odd)(out_gradient_back)

    back_to[...] = differentiate(1, far, project(far, lambda c: send_x(c).wait_recv()), received_att, nxt)
    send_back.start()

    def start_sums(k, first, last):
        @pl.when((d == 0) & (k > 0))
        def _():
            for p in range(first, last):
                send_up(k, p).start()

        @pl.when((d == n - 1) & (k < n - 1))
        def _():
            for p in range(first, last):
                send_down(k, p).start()

    def gradient_qkv(i, carry):
        k = shard_at(i)
        gt[k, :cols, :] = dot(dt[...], xx[:, lanes(k)]).astype(BF16)
        start_sums(k, 0, PARTS - 1)
        return carry

    lax.fori_loop(0, n, gradient_qkv, 0)
    pl.when(even)(answer)

    def far_term(c, carry):
        tsend[:, lanes(c)] = dot_nt(dq[1], w[lanes(c), :]).astype(BF16)
        send_term(c).start()
        return carry

    lax.fori_loop(0, n // 2, far_term, 0)

    def other_half():
        lax.fori_loop(n // 2, n, far_term, 0)

    def pass_on(t, first, each):
        up, down = t - d, t - (n - 1 - d)

        @pl.when((d > 0) & (up >= 0) & (up < (n - 1 - d) * each))
        def _():
            k, p = n - 1 - up // each, first + up % each
            send_up(k, p).wait_recv()
            gt[k, rows(p), :] = (gt[k, rows(p), :].astype(F32) + from_low[k, rows(p), :].astype(F32)).astype(BF16)
            send_up(k, p).start()

        @pl.when((d < n - 1) & (down >= 0) & (down < d * each))
        def _():
            k, p = down // each, first + down % each
            send_down(k, p).wait_recv()
            gt[k, rows(p), :] = (gt[k, rows(p), :].astype(F32) + from_high[k, rows(p), :].astype(F32)).astype(BF16)
            send_down(k, p).start()

    ticks = 1 + (n - 2) * (PARTS - 1)

    between = (d > 0) & (d < n - 1)

    def tick_qkv(t, carry):
        pl.when(between & (t == (1 + ticks) // 2))(other_half)
        pass_on(t, 0, PARTS - 1)
        return carry

    lax.fori_loop(1, ticks, tick_qkv, 0)

    def own_term(c, carry):
        term[:, lanes(c)] = dot_nt(dq[0], w[lanes(c), :])
        return carry

    lax.fori_loop(0, n, own_term, 0)

    pl.when(even)(out_gradient_back)

    def gradient_out(i, carry):
        k = shard_at(i)
        send_go(k).wait_recv()
        gt[k, cols:, :] = (dot(turned_att[...], gg[:, lanes(k)]) + go_from[:, lanes(k)].astype(F32)).astype(BF16)
        start_sums(k, PARTS - 1, PARTS)
        return carry

    lax.fori_loop(0, n, gradient_out, 0)
    pl.when(jnp.logical_not(between))(other_half)

    def tick_out(t, carry):
        pass_on(t, PARTS - 1, 1)
        return carry

    lax.fori_loop(1, n - 1, tick_out, 0)

    def store(c):
        return pltpu.make_async_copy(tback.at[:, lanes(c)], ig_hbm.at[:, lanes(c)], store_sem.at[c])

    def finish_input(c, carry):
        send_term(c).wait_recv()
        tback[:, lanes(c)] = (term[:, lanes(c)] + tback[:, lanes(c)].astype(F32)).astype(BF16)
        store(c).start()
        return carry

    lax.fori_loop(0, n, finish_input, 0)

    for p in range(PARTS):
        pl.when(d > 0)(lambda p=p: send_up(d, p).wait_recv())
        pl.when(d < n - 1)(lambda p=p: send_down(d, p).wait_recv())
        total = gt[d, rows(p), :].astype(F32)
        total += jnp.where(d > 0, from_low[d, rows(p), :].astype(F32), F32(0.0))
        total += jnp.where(d < n - 1, from_high[d, rows(p), :].astype(F32), F32(0.0))
        if p < PARTS - 1:
            turned[:, rows(p)] = total.T.astype(BF16)
        else:
            plain[...] = total.astype(BF16)

    send_wo.wait_send()
    send_att.wait_send()
    send_back.wait_send()
    for c in range(n):
        send_x(c).wait_send()
        send_go(c).wait_send()
        send_term(c).wait_send()
        store(c).wait()
        for p in range(PARTS):

            @pl.when(d < c)
            def _(c=c, p=p):
                send_up(c, p).wait_send()

            @pl.when(d > c)
            def _(c=c, p=p):
                send_down(c, p).wait_send()


def place_kernel(n, wide, ig_hbm, qkv_hbm, out_hbm, ig_to, qkv_to, out_to, ig, qkv, out, sem):
    def lanes(c):
        return pl.ds(c * wide, wide)

    legs = [(ig_hbm.at[:, lanes(c)], ig.at[:, lanes(c)], ig_to.at[:, lanes(c)]) for c in range(n)]
    legs += [(qkv_hbm, qkv, qkv_to), (out_hbm, out, out_to)]
    reads = [pltpu.make_async_copy(src, mid, sem.at[0, i]) for i, (src, mid, _) in enumerate(legs)]
    writes = [pltpu.make_async_copy(mid, dst, sem.at[1, i]) for i, (_, mid, dst) in enumerate(legs)]
    for read in reads:
        read.start()
    for read, write in zip(reads, writes):
        read.wait()
        write.start()
    for write in writes:
        write.wait()


def spread(array, dim, n, wide):
    shape = array.shape
    each = shape[dim] // n
    if each == wide:
        return array
    split = array.reshape(shape[:dim] + (n, each) + shape[dim + 1 :])
    pads = [(0, 0)] * split.ndim
    pads[dim + 1] = (0, wide - each)
    return jnp.pad(split, pads).reshape(shape[:dim] + (n * wide,) + shape[dim + 1 :])


def local(normed_input, segment_ids, weights_qkv, weights_out, cotangent):
    nb, n = lax.axis_size("blk"), lax.axis_size("dp")
    _, count, depth = normed_input.shape
    head = weights_out.shape[1]
    each = depth // n
    wide = -(-each // 128) * 128
    full = n * wide
    rows = 4 * head
    hbm = pl.BlockSpec(memory_space=pl.ANY)
    vmem = pl.BlockSpec(memory_space=pltpu.VMEM)
    dma = pltpu.SemaphoreType.DMA
    seq = pltpu.VMEM((count, full), BF16)
    pairs = pltpu.VMEM((2 * count, full), BF16)
    heads = pltpu.VMEM((head, full), BF16)
    shards = pltpu.VMEM((n, rows, wide), BF16)
    results = (
        jax.ShapeDtypeStruct((count, full), BF16),
        jax.ShapeDtypeStruct((wide, 3 * head), BF16),
        jax.ShapeDtypeStruct((head, wide), BF16),
    )
    made = pl.pallas_call(
        functools.partial(kernel, nb, n, wide),
        out_shape=results,
        in_specs=[hbm, hbm, vmem, hbm, hbm],
        out_specs=(hbm, vmem, vmem),
        scratch_shapes=[
            pairs, seq,
            pltpu.VMEM((full, 3 * head), BF16),
            heads, heads, heads, heads,
            pltpu.VMEM((count, head), BF16),
            pltpu.VMEM((count, head), BF16),
            pltpu.VMEM((head, count), BF16),
            pltpu.VMEM((head, count), BF16),
            pltpu.VMEM((head, count), BF16),
            pltpu.VMEM((3 * head, 2 * count), BF16),
            pltpu.VMEM((2, count, 3 * head), BF16),
            shards, shards, shards,
            pltpu.VMEM((count, full), F32),
            seq, seq,
            dma((4,)), dma((n,)), dma((n,)), dma((n,)), dma((n,)), dma((2,)), dma((2,)), dma((2,)), dma((n,)), dma((n,)),
            dma((n, PARTS)), dma((n, PARTS)), dma((n, PARTS)), dma((n, PARTS)), dma((n,)),
        ],
        compiler_params=pltpu.CompilerParams(
            collective_id=0, has_side_effects=True, vmem_limit_bytes=60 * 1024 * 1024
        ),
    )(
        spread(normed_input[0], 1, n, wide),
        spread(cotangent[0], 1, n, wide),
        segment_ids[0],
        spread(weights_qkv[0], 0, n, wide),
        spread(weights_out[0], 1, n, wide),
    )
    input_grad, grad_qkv, grad_out = pl.pallas_call(
        functools.partial(place_kernel, n, wide),
        out_shape=results,
        in_specs=[hbm, hbm, hbm],
        out_specs=(hbm, hbm, hbm),
        scratch_shapes=[pltpu.VMEM(made_one.shape, BF16) for made_one in results] + [dma((2, n + 2))],
        compiler_params=pltpu.CompilerParams(vmem_limit_bytes=60 * 1024 * 1024),
    )(*made)
    if each != wide:
        input_grad = input_grad.reshape(count, n, wide)[:, :, :each].reshape(count, depth)
    return input_grad[None], grad_qkv[None, :each], grad_out[None, :, :each]


def solution(mesh):
    placed = (
        P(("blk", "dp"), None, None),
        P("dp", None, None),
        P("blk", None, None),
        P("blk", None, None),
        P(("blk", "dp"), None, None),
    )
    return jax.shard_map(
        local,
        mesh=mesh,
        in_specs=placed,
        out_specs=(P(("blk", "dp"), None, None), P("blk", "dp", None), P("blk", None, "dp")),
        check_vma=False,
    )
```
